256 devices in a mesh: row: 8 (over y, z_hi), col: 32 (over x, z_lo, core).
Axes of the slice: x: 4, y: 4, z: 8 (z_hi: 2, z_lo: 4; z = z_hi * 4 + z_lo), core: 2. Of those that a mesh axis runs over, the one named last changes fastest.
Arguments:
- matrix: bfloat16 [16384, 16384], P('row', 'col'), may hold values from 0 to 250, as said below
- pivots: int32 [512], replicated, may hold values from 0 to 16383, as said below
- lower_inverse: bfloat16 [512, 512], replicated, may hold values from 0 to 250, as said below
- upper_inverse: bfloat16 [512, 512], replicated, may hold values from 0 to 250, as said below
Outputs:
- factored: float32 [16384, 16384], P('row', 'col')
The draws below stay inside these ranges and needn't reach their ends.
Inputs may be any that keep to these rules, and one draw needn't show every extreme that they name: The entries are distinct; pivots[j] is either j or a row of 512 to 16383. `matrix`: integers 0 to 250. `lower_inverse`: integers 0 to 250, unit lower triangular. `upper_inverse`: integers 0 to 250, upper triangular with diagonal 1 to 250.
All inputs are finite; a program needn't handle non-finite values.
Results may differ from the reference program's by a relative error of at most 0.0003.
Values may be sent and summed in bfloat16 or wider, within the bound.
A program may use at most 64 MiB of HBM per device.

```python
import jax
import jax.numpy as jnp
from jax import lax

N = 16384
PANEL = 512
DEPTH = 128


def draw_matrix(key, part):
    key = jax.random.fold_in(key, 1)
    values = jax.random.randint(key, (N, N), 0, 251)
    return values.astype(jnp.float32).astype(jnp.bfloat16)


def draw_pivots(key, part):
    key = jax.random.fold_in(key, 2)
    first_key, second_key = jax.random.split(key)
    rows = jax.random.permutation(first_key, N - PANEL - 1)[:PANEL].astype(jnp.int32) + PANEL
    rows = rows.at[PANEL - 1].set(N - 1)
    keep = jax.random.randint(second_key, (PANEL,), 0, 4) == 0
    keep = keep.at[0].set(True).at[PANEL - 1].set(False)
    return jnp.where(keep, jnp.arange(PANEL, dtype=jnp.int32), rows)


def draw_lower_inverse(key, part):
    key = jax.random.fold_in(key, 3)
    values = jax.random.randint(key, (PANEL, PANEL), 0, 251).astype(jnp.float32)
    lower = jnp.tril(values, -1) + jnp.eye(PANEL, dtype=jnp.float32)
    return lower.astype(jnp.bfloat16)


def draw_upper_inverse(key, part):
    key = jax.random.fold_in(key, 4)
    first_key, second_key = jax.random.split(key)
    values = jax.random.randint(first_key, (PANEL, PANEL), 0, 251).astype(jnp.float32)
    diag_values = jax.random.randint(second_key, (PANEL,), 1, 251).astype(jnp.float32)
    upper = jnp.triu(values, 1) + jnp.diag(diag_values)
    return upper.astype(jnp.bfloat16)


def setup_inputs(seed: int = 0) -> dict:
    key_list = jax.random.split(jax.random.key(seed), 5)
    matrix = draw_matrix(jax.random.fold_in(key_list[4], 71), 0)
    pivots = draw_pivots(jax.random.fold_in(key_list[4], 71), 0)
    lower_inverse = draw_lower_inverse(jax.random.fold_in(key_list[4], 71), 0)
    upper_inverse = draw_upper_inverse(jax.random.fold_in(key_list[4], 71), 0)
    return {"matrix": matrix, "pivots": pivots, "lower_inverse": lower_inverse, "upper_inverse": upper_inverse}


def reduce_mod(x):
    quot = jnp.floor(x * (1.0 / 251.0))
    rest = x - quot * 251.0
    rest = jnp.where(rest < 0, rest + 251.0, rest)
    return jnp.where(rest >= 251.0, rest - 251.0, rest)


def product_mod(left, right):
    steps = left.shape[1] // DEPTH
    total = jnp.zeros((left.shape[0], right.shape[1]), left.dtype)
    for step in range(steps):
        part = jnp.dot(left[:, step * DEPTH:(step + 1) * DEPTH], right[step * DEPTH:(step + 1) * DEPTH], precision=lax.Precision.HIGHEST)
        total = total + reduce_mod(part)
    return reduce_mod(total)


def reference(matrix, pivots, lower_inverse, upper_inverse):
    whole = matrix.astype(jnp.float32)
    first = jnp.arange(PANEL, dtype=jnp.int32)
    order = jnp.arange(N, dtype=jnp.int32).at[first].set(pivots).at[pivots].set(first)
    swapped = whole[order]
    linv = lower_inverse.astype(jnp.float32)
    uinv = upper_inverse.astype(jnp.float32)
    upper_block = product_mod(linv, swapped[:PANEL, PANEL:])
    lower_block = product_mod(swapped[PANEL:, :PANEL], uinv)
    blocks = (N - PANEL) // PANEL
    rest = swapped[PANEL:, PANEL:].reshape(blocks, PANEL, N - PANEL)
    lower_parts = lower_block.reshape(blocks, PANEL, PANEL)
    trailing = lax.map(lambda pair: reduce_mod(pair[0] - product_mod(pair[1], upper_block)), (rest, lower_parts))
    trailing = trailing.reshape(N - PANEL, N - PANEL)
    top = jnp.concatenate([swapped[:PANEL, :PANEL], upper_block], axis=1)
    bottom = jnp.concatenate([lower_block, trailing], axis=1)
    return jnp.concatenate([top, bottom], axis=0) / 251.0
```

```python
import functools

import jax
import jax.numpy as jnp
from jax import lax
from jax.experimental import pallas as pl
from jax.experimental.pallas import tpu as pltpu
from jax.sharding import PartitionSpec as P

MESH = pl.DeviceIdType.MESH
PRIME = 251.0
INVERSE = 1.0 / 251.0
NY, NX, NZ = 4, 4, 4


def residue(x):
    rest = x - jnp.floor(x * INVERSE + 0.5) * PRIME
    return jnp.where(rest < 0, rest + PRIME, rest)


def balanced(x):
    return x - jnp.floor(x * INVERSE + 0.5) * PRIME


def dot(a, b):
    return jnp.dot(a, b, preferred_element_type=jnp.float32)


def exchange_kernel(
    piv_ref, s_ref, pf, cf, tt, xf, pcol, oh, g, r1, zs, r2, msg,
    raw_send, raw_recv, cor_send, cor_recv, src_send, row_send, row_recv, loc,
):
    rows = s_ref.shape[0]
    panel = xf.shape[0]
    piece = rows // (NX * NZ)
    small = panel // (NX * NZ)
    part = panel // NY
    r = lax.axis_index("row")
    c = lax.axis_index("col")
    y, h = r // 2, r % 2
    x, z, k = c // 8, (c // 2) % 4, c % 2
    me = x * NZ + z

    def chip(x2, z2, k2=0):
        return {"row": r, "col": x2 * 8 + z2 * 2 + k2}

    def along(y2, h2):
        return {"row": y2 * 2 + h2, "col": c}

    def signal(device):
        pl.semaphore_signal(barrier, 1, device_id=device, device_id_type=MESH)

    barrier = pltpu.get_barrier_semaphore()
    for step in range(1, 8):
        signal({"row": (r + step) % 8, "col": c})
    signal(chip(x, z, 1 - k))

    @pl.when(k == 0)
    def _():
        for step in range(1, NX * NZ):
            other = (me + step) % (NX * NZ)
            signal(chip(other // NZ, other % NZ))

    @pl.when(k == 0)
    def _():
        pl.semaphore_wait(barrier, 7 + NX * NZ)

    @pl.when(k == 1)
    def _():
        pl.semaphore_wait(barrier, 8)

    def remote(src, dst, send, recv, device):
        return pltpu.make_async_remote_copy(
            src_ref=src, dst_ref=dst, send_sem=send, recv_sem=recv,
            device_id=device, device_id_type=MESH,
        )

    def raw(p, slot, device, source=None):
        ref = pf if source is None else source
        return remote(
            ref.at[pl.ds(p * piece, piece)], pf.at[pl.ds(p * piece, piece)],
            raw_send.at[slot], raw_recv.at[p], device,
        )

    def cor(p, slot, device, source=None):
        ref = cf if source is None else source
        return remote(
            ref.at[pl.ds(p * small, small)], cf.at[pl.ds(p * small, small)],
            cor_send.at[slot], cor_recv.at[p], device,
        )

    is_core = k == 0
    is_src = (k == 0) & (me == 0)
    is_first = is_src & (r == 0)
    own_copy = pltpu.make_async_copy(s_ref, pf, loc.at[0])
    cor_copy = pltpu.make_async_copy(s_ref.at[pl.ds(0, small)], cf.at[pl.ds(0, small)], loc.at[1])

    def first_cor(p):
        return remote(
            s_ref.at[pl.ds(p * small, small)], cf.at[pl.ds(p * small, small)],
            src_send.at[16 + p], cor_recv.at[p], chip(p // NZ, p % NZ),
        )

    def first_raw(p):
        return remote(
            s_ref.at[pl.ds(p * piece, piece)], pf.at[pl.ds(p * piece, piece)],
            src_send.at[p], raw_recv.at[p], chip(p // NZ, p % NZ),
        )

    def core_raw(p):
        return remote(
            pf.at[pl.ds(p * piece, piece)], pf.at[pl.ds(p * piece, piece)],
            src_send.at[32 + p], raw_recv.at[p], chip(x, z, 1),
        )

    def core_src(p):
        return remote(
            s_ref.at[pl.ds(p * piece, piece)], pf.at[pl.ds(p * piece, piece)],
            src_send.at[32 + p], raw_recv.at[p], chip(x, z, 1),
        )

    core_cor = remote(cf, cf, src_send.at[48], loc.at[2], chip(x, z, 1))
    order = (8, 4, 12, 1, 9, 5, 13, 2, 10, 6, 14, 3, 11, 7, 15)

    @pl.when(is_first)
    def _():
        cor_copy.start()
        for p in order:
            first_cor(p).start()

    @pl.when(is_src)
    def _():
        for p in order:
            first_raw(p).start()
        own_copy.start()
        for p in range(16):
            core_src(p).start()

    lane = lax.broadcasted_iota(jnp.int32, (panel, 128), 1)
    for t in range(panel // 128):
        line = jnp.broadcast_to(piv_ref[:, t * 128 : (t + 1) * 128], (128, 128))
        pcol[t * 128 : (t + 1) * 128, :] = jnp.transpose(line)
    named = pcol[...]

    def build(t, carry):
        hit = named == lane + (r * rows + t * 128)
        oh[:, pl.ds(pl.multiple_of(t * 128, 128), 128)] = jnp.where(hit, 1.0, 0.0).astype(jnp.bfloat16)
        return carry

    lax.fori_loop(0, rows // 128, build, 0)

    def owner_of(start, size):
        return pcol[pl.ds(start, size), :] // rows

    def wide(mask_value, width):
        return jnp.concatenate([mask_value] * (width // 128), axis=1)

    def pick(t, carry):
        start = pl.multiple_of(t * 256, 256)
        picked = dot(oh[pl.ds(start, 256), :], s_ref[...])
        owner = wide(owner_of(start, 256), panel)
        old = s_ref[pl.ds(start, 256), :].astype(jnp.float32)
        use = (owner * jnp.where(r == 0, 1, 0)) == 0
        g[pl.ds(start, 256), :] = jnp.where(use, picked, old).astype(jnp.bfloat16)
        return carry

    lax.fori_loop(0, panel // 256, pick, 0)

    def one(d):
        y2 = (y + d) % NY
        return remote(
            g.at[pl.ds(pl.multiple_of(y2 * part, part), part)], r1.at[d - 1],
            row_send.at[d - 1], row_recv.at[d - 1], along(y2, h),
        )

    def two():
        return remote(zs, r2, row_send.at[3], row_recv.at[3], along(y, 1 - h))

    def three(d):
        return remote(
            msg.at[d - 1], xf.at[pl.ds(pl.multiple_of(y * part, part), part)],
            row_send.at[3 + d], row_recv.at[3 + d], along((y + d) % NY, h),
        )

    def three_in(d):
        return remote(
            msg.at[d - 1], xf.at[pl.ds(pl.multiple_of(((y + NY - d) % NY) * part, part), part)],
            row_send.at[3 + d], row_recv.at[3 + d], along((y + d) % NY, h),
        )

    for d in (2, 1, 3):
        one(d).start()

    def spread_raw_x(p, slot):
        for step in range(1, NX):
            raw(p, slot + step - 1, chip((x + step) % NX, z)).start()

    def spread_cor_x(p, slot):
        for step in range(1, NX):
            cor(p, slot + step - 1, chip((x + step) % NX, z)).start()

    @pl.when(is_core & (me != 0))
    def _():
        raw(me, 0, chip(x, z)).wait_recv()
        for step in range(1, NZ):
            z2 = (z + step) % NZ

            @pl.when((x > 0) | (z2 > 0))
            def _():
                raw(me, step - 1, chip(x, z2)).start()

        for step in range(1, NX):
            x2 = (x + step) % NX

            @pl.when((z > 0) | (x2 > 0))
            def _():
                raw(me, 2 + step, chip(x2, z)).start()

        @pl.when(x == 0)
        def _():
            for step in range(1, NX):
                raw(me, 14 + step, chip(step, 0)).start()

        core_raw(me).start()

    @pl.when(is_src)
    def _():
        for step in range(1, NZ):
            raw(0, step - 1, chip(0, step), s_ref).start()
        for step in range(1, NX):
            raw(0, 2 + step, chip(step, 0), s_ref).start()

    def own_cor():
        for step in range(1, NZ):
            cor(me, step - 1, chip(x, (z + step) % NZ)).start()
        spread_cor_x(me, 3)

    def down(step):
        return remote(
            cf.at[pl.ds(me * small, small)], cf.at[pl.ds(me * small, small)],
            cor_send.at[14 + step], cor_recv.at[me], {"row": step, "col": c},
        )

    @pl.when(is_first)
    def _():
        cor_copy.wait()

    @pl.when(is_core & (r == 0) & (me != 0))
    def _():
        cor(me, 0, chip(x, z)).wait_recv()

    @pl.when(is_core & (r == 0))
    def _():
        for step in range(1, 8):
            down(step).start()
        own_cor()

    def halves():
        home = pl.ds(pl.multiple_of(y * part, part), part)
        owner = wide(owner_of(pl.multiple_of(y * part, part), part), panel)
        first = jnp.zeros((part, panel), jnp.float32)
        rest = jnp.zeros((part, panel), jnp.float32)
        for d in range(NY):
            got = (g[home, :] if d == 0 else r1[d - 1]).astype(jnp.float32)
            flag = jnp.where(((y + NY - d) % NY == 0) & (h == 0), 1.0, 0.0)
            first = first + got * flag
            rest = rest + got * (1.0 - flag)
        return owner, first, rest

    for d in (1, 3, 2):
        one(d).wait_recv()
    owner, first, rest = halves()
    low = jnp.where(h == 0, 1, 0)
    away = (owner % 2 == 0) & (owner != 0)
    zs[...] = jnp.where(away | (owner * low != owner), rest, jnp.where(low == 1, first, rest)).astype(jnp.bfloat16)
    two().start()

    @pl.when(is_core & (me != 0))
    def _():
        for step in range(1, NZ):
            z2 = (z + step) % NZ
            p = x * NZ + z2
            raw(p, 0, chip(x, z)).wait_recv()
            for leap in range(1, NX):
                x2 = (x + leap) % NX

                @pl.when((z > 0) | (x2 > 0))
                def _():
                    raw(p, 3 + 3 * step + leap - 1, chip(x2, z)).start()

            core_raw(p).start()

    @pl.when(is_core & (r != 0))
    def _():
        cor(me, 0, chip(x, z)).wait_recv()
        own_cor()

    @pl.when(is_core)
    def _():
        for step in range(1, NZ):
            p = x * NZ + (z + step) % NZ
            cor(p, 0, chip(x, z)).wait_recv()
            spread_cor_x(p, 3 + 3 * step)

    two().wait_recv()
    owner, first, rest = halves()
    got = r2[...].astype(jnp.float32)
    odd = owner % 2 == 1
    low_t = jnp.where(odd, got, jnp.where(owner == 0, first, rest))
    high_t = jnp.where(odd, rest, got)
    flag = jnp.where(h == 0, 1.0, 0.0)
    new = low_t * flag + high_t * (1.0 - flag)
    old = first * flag + got * (1.0 - flag)
    for d in (2, 1, 3):
        y2 = (y + d) % NY
        msg[d - 1] = jnp.where(owner == y2 * 2 + h, old, new).astype(jnp.bfloat16)
        three(d).start()
    xf[pl.ds(pl.multiple_of(y * part, part), part), :] = jnp.where(owner == r, old, new).astype(jnp.bfloat16)

    @pl.when(is_core & (me != 0))
    def _():
        for leap in range(1, NX):
            x2 = (x + leap) % NX
            for z2 in range(NZ):
                p = x2 * NZ + z2
                raw(p, 0, chip(x, z)).wait_recv()
                core_raw(p).start()

    @pl.when(is_core)
    def _():
        for leap in range(1, NX):
            x2 = (x + leap) % NX
            for z2 in range(NZ):
                cor(x2 * NZ + z2, 0, chip(x, z)).wait_recv()
        core_cor.start()

    for d in (1, 3, 2):
        three_in(d).wait_recv()

    def finish(t, carry):
        start = pl.multiple_of(t * 128, 128)
        owner = wide(owner_of(start, 128), panel)
        mine = g[pl.ds(start, 128), :].astype(jnp.float32)
        got = xf[pl.ds(start, 128), :].astype(jnp.float32)
        tt[pl.ds(start, 128), :] = jnp.where(owner == r, mine, got).astype(jnp.bfloat16)
        return carry

    lax.fori_loop(0, panel // 128, finish, 0)

    @pl.when(r == 0)
    def _():
        xf[...] = s_ref[0:panel, :]

    for d in (1, 2, 3):
        one(d).wait_send()
        three(d).wait_send()
    two().wait_send()

    @pl.when(k == 1)
    def _():
        for p in range(16):
            raw(p, 0, chip(x, z)).wait_recv()
        core_cor.wait_recv()

    @pl.when(is_src)
    def _():
        own_copy.wait()
        for p in order:
            first_raw(p).wait_send()
        for p in range(16):
            core_src(p).wait_send()
        for slot in range(6):
            raw(0, slot, chip(x, z)).wait_send()

    @pl.when(is_first)
    def _():
        for p in order:
            first_cor(p).wait_send()

    @pl.when(is_core & (r == 0))
    def _():
        for step in range(1, 8):
            down(step).wait_send()

    @pl.when(is_core)
    def _():
        for slot in range(15):
            cor(0, slot, chip(x, z)).wait_send()
        core_cor.wait_send()

    @pl.when(is_core & (me != 0))
    def _():
        for step in range(1, NZ):
            @pl.when((x > 0) | ((z + step) % NZ > 0))
            def _():
                raw(0, step - 1, chip(x, z)).wait_send()

        for step in range(4):
            for leap in range(1, NX):
                @pl.when((z > 0) | ((x + leap) % NX > 0))
                def _():
                    raw(0, 3 + 3 * step + leap - 1, chip(x, z)).wait_send()

        @pl.when(x == 0)
        def _():
            for step in range(1, NX):
                raw(0, 14 + step, chip(x, z)).wait_send()

        for p in range(16):
            core_raw(p).wait_send()


def exchange(piv, s, panel):
    rows, cols = s.shape
    part = panel // NY
    bf = jnp.bfloat16
    dma = pltpu.SemaphoreType.DMA
    vmem = pl.BlockSpec(memory_space=pltpu.VMEM)
    return pl.pallas_call(
        exchange_kernel,
        out_shape=[
            jax.ShapeDtypeStruct((rows, panel), bf),
            jax.ShapeDtypeStruct((panel, panel), bf),
            jax.ShapeDtypeStruct((panel, cols), bf),
            jax.ShapeDtypeStruct((panel, cols), bf),
        ],
        in_specs=[vmem, vmem],
        out_specs=[vmem] * 4,
        scratch_shapes=[
            pltpu.VMEM((panel, 128), jnp.int32),
            pltpu.VMEM((panel, rows), bf),
            pltpu.VMEM((panel, cols), bf),
            pltpu.VMEM((NY - 1, part, cols), bf),
            pltpu.VMEM((part, cols), bf),
            pltpu.VMEM((part, cols), bf),
            pltpu.VMEM((NY - 1, part, cols), bf),
            dma((18,)), dma((16,)), dma((22,)), dma((16,)), dma((49,)), dma((7,)), dma((7,)), dma((3,)),
        ],
        compiler_params=pltpu.CompilerParams(
            collective_id=0, has_side_effects=True, vmem_limit_bytes=48 << 20
        ),
        name="exchange",
    )(piv, s)


def update_kernel(piv_ref, s_ref, p_ref, cf, tt, xf, linv, uinv, o_ref, w, rep, top):
    tile = s_ref.shape[0]
    panel = w.shape[0]
    step = pl.program_id(0)
    r = lax.axis_index("row")
    c = lax.axis_index("col")
    bf = jnp.bfloat16
    left = jnp.where(c == 0, 1.0, 0.0)

    @pl.when(step == 0)
    def _():
        ub = balanced(uinv[...].astype(jnp.float32)).astype(bf)
        lb = balanced(linv[...].astype(jnp.float32)).astype(bf)
        new = tt[...]
        both = balanced(dot(ub, lb)).astype(bf)
        right = balanced(dot(both, new))
        w[...] = jnp.where(c == 0, -ub.astype(jnp.float32), right).astype(bf)
        old = jnp.where(c == 0, 0.0, xf[...].astype(jnp.float32))
        rep[...] = (residue(old - dot(cf[...], w[...])) + 1.0).astype(bf)

        @pl.when(r == 0)
        def _():
            upper = residue(dot(lb, new))
            top[...] = jnp.where(c == 0, new.astype(jnp.float32), upper) * INVERSE

    rows = lax.broadcasted_iota(jnp.int32, (tile, panel), 0) + (
        r * (tile * pl.num_programs(0)) + step * tile
    )
    hit = jnp.where(rows == piv_ref[...], 1.0, 0.0).astype(bf)
    swapped = dot(hit, rep[...])
    raw = jnp.where(c == 0, 0.0, s_ref[...].astype(jnp.float32))
    rest = residue(raw - dot(p_ref[...], w[...]))
    o_ref[...] = jnp.where(swapped > 0, swapped - 1.0, rest) * INVERSE

    @pl.when((r == 0) & (step * tile < panel))
    def _():
        o_ref[...] = top[pl.ds(pl.multiple_of(step * tile, tile), tile), :]


def update(piv, s, pf, cf, tt, xf, linv, uinv):
    rows, cols = s.shape
    panel = cf.shape[0]
    tile = 256
    whole = lambda shape: pl.BlockSpec(shape, lambda i: (0, 0))
    tiled = pl.BlockSpec((tile, cols), lambda i: (i, 0))
    square = whole((panel, panel))
    return pl.pallas_call(
        update_kernel,
        grid=(rows // tile,),
        out_shape=jax.ShapeDtypeStruct((rows, cols), jnp.float32),
        in_specs=[whole((1, panel)), tiled, pl.BlockSpec((tile, panel), lambda i: (i, 0))] + [square] * 5,
        out_specs=tiled,
        scratch_shapes=[
            pltpu.VMEM((panel, cols), jnp.bfloat16),
            pltpu.VMEM((panel, cols), jnp.bfloat16),
            pltpu.VMEM((panel, cols), jnp.float32),
        ],
        compiler_params=pltpu.CompilerParams(vmem_limit_bytes=48 << 20),
        name="update",
    )(piv, s, pf, cf, tt, xf, linv, uinv)


def per_device(matrix, pivots, lower_inverse, upper_inverse):
    panel = lower_inverse.shape[0]
    piv = pivots.reshape(1, panel)
    pf, cf, tt, xf = exchange(piv, matrix, panel)
    return update(piv, matrix, pf, cf, tt, xf, lower_inverse, upper_inverse)


def solution(mesh):
    placed = (P("row", "col"), P(), P(), P())
    return jax.shard_map(
        per_device, mesh=mesh, in_specs=placed, out_specs=P("row", "col"), check_vma=False
    )
```

```python
import functools

import jax
import jax.numpy as jnp
from jax import lax
from jax.experimental import pallas as pl
from jax.experimental.pallas import tpu as pltpu
from jax.sharding import PartitionSpec as P

MESH = pl.DeviceIdType.MESH
PRIME = 251.0
INVERSE = 1.0 / 251.0
ROUND = 1.5 * 2.0**23
NY, NX, NZ = 4, 4, 4
CHUNKS = 2
FIX = 4


def balanced(x):
    quot = (x * INVERSE + ROUND) - ROUND
    return x - quot * PRIME


def residue(x):
    rest = balanced(x)
    return jnp.where(rest < 0, rest + PRIME, rest)


def dot(a, b):
    return jnp.dot(a, b, preferred_element_type=jnp.float32)


def exchange_kernel(
    piv_hbm, linv_hbm, uinv_hbm, s_hbm, o_hbm, piv_ref, linv, uinv, out, pf, tt, xf, both, wk, rep, s_ref, pcol, oh, g, r1, zs, r2, msg,
    net_send, net_recv, src_send, src_recv, core_send, core_recv, down_send, row_send, row_recv, loc, out_sem,
):
    rows = s_ref.shape[0]
    panel = xf.shape[0]
    half = rows // 2
    line = half // NX
    piece = line // 4
    fix = panel // 2
    part = panel // NY
    r = lax.axis_index("row")
    c = lax.axis_index("col")
    y, h = r // 2, r % 2
    x, z, k = c // 8, (c // 2) % 4, c % 2
    first_plane = z == 0
    is_src = first_plane & (x == 0)
    loads = [
        pltpu.make_async_copy(src, dst, loc.at[2 + i])
        for i, (src, dst) in enumerate(
            ((piv_hbm, piv_ref), (s_hbm, s_ref), (uinv_hbm, uinv), (linv_hbm, linv))
        )
    ]
    for load in loads:
        load.start()

    def chip(x2, z2):
        return {"row": r, "col": x2 * 8 + z2 * 2 + k}

    def along(y2, h2):
        return {"row": y2 * 2 + h2, "col": c}

    sibling = {"row": r, "col": c + 1 - 2 * k}
    barrier = pltpu.get_barrier_semaphore()

    def signal(device):
        pl.semaphore_signal(barrier, 1, device_id=device, device_id_type=MESH)

    signal(sibling)
    for step in range(1, 4):
        signal(chip((x + step) % NX, z))
        signal(chip(x, (z + step) % NZ))
    for step in range(1, 8):
        signal({"row": (r + step) % 8, "col": c})

    def remote(src, dst, send, recv, device):
        return pltpu.make_async_remote_copy(
            src_ref=src, dst_ref=dst, send_sem=send, recv_sem=recv,
            device_id=device, device_id_type=MESH,
        )

    def place(q, t):
        if isinstance(t, int) and t == FIX:
            return pl.ds(pl.multiple_of(rows + k * fix + q * piece, piece), piece)
        return pl.ds(pl.multiple_of(k * half + t * line + q * piece, piece), piece)

    def net(q, t, slot, device):
        return remote(
            pf.at[place(q, t)], pf.at[place(q, t)], net_send.at[slot], net_recv.at[q * 5 + t], device
        )

    def arrived(q, t):
        net(q, t, 0, sibling).wait_recv()

    def sent(slot):
        net(0, 0, slot, sibling).wait_send()

    def src_piece(ref, q, t, slot, device):
        return remote(
            ref.at[place(q, t)], pf.at[place(q, t)], src_send.at[slot], net_recv.at[q * 5 + t], device
        )

    def line_place(k2, q):
        return pl.ds(pl.multiple_of(k2 * half + q * line, line), line)

    def core_line(q):
        return remote(
            pf.at[line_place(k, q)], pf.at[line_place(k, q)], core_send.at[q], core_recv.at[q], sibling
        )

    def core_line_in(q):
        return remote(
            pf.at[line_place(1 - k, q)], pf.at[line_place(1 - k, q)],
            core_send.at[q], core_recv.at[q], sibling,
        )

    def fix_place(k2):
        return pl.ds(pl.multiple_of(rows + k2 * fix, fix), fix)

    def core_fix():
        return remote(
            pf.at[fix_place(k)], pf.at[fix_place(k)], core_send.at[4], core_recv.at[4], sibling
        )

    def core_fix_in():
        return remote(
            pf.at[fix_place(1 - k)], pf.at[fix_place(1 - k)],
            core_send.at[4], core_recv.at[4], sibling,
        )

    def give(k2, q):
        at = pl.ds(k2 * half + q * line, line)
        return remote(
            s_hbm.at[at], pf.at[at], src_send.at[16 + k2 * 4 + q],
            src_recv.at[q] if k2 else core_recv.at[q], sibling,
        )

    def give_fix():
        return remote(
            s_hbm.at[pl.ds(fix, fix)], pf.at[pl.ds(rows + fix, fix)],
            src_send.at[24], src_recv.at[4], sibling,
        )

    own_copy = pltpu.make_async_copy(s_hbm, pf.at[pl.ds(0, rows)], loc.at[0])
    own_fix = pltpu.make_async_copy(s_hbm.at[pl.ds(0, fix)], pf.at[pl.ds(rows, fix)], loc.at[1])

    def fix_out(q, slot):
        return remote(
            pf.at[place(q, 4)], pf.at[place(q, 4)], src_send.at[slot], net_recv.at[q * 5 + 4], chip(q, 0)
        )

    def down(step):
        return remote(
            pf.at[place(x, FIX)], pf.at[place(x, FIX)], down_send.at[step // 2 if isinstance(step, int) else 0],
            net_recv.at[x * 5 + FIX], {"row": step, "col": c},
        )

    plan = (
        (2, 0, 2, 0), (3, 0, 3, 0), (0, 0, 0, 1), (1, 0, 1, 0), (2, 2, 3, 0), (0, 1, 0, 1),
        (2, 1, 2, 0), (3, 1, 3, 0), (1, 1, 1, 0), (2, 3, 3, 0), (0, 2, 0, 1),
        (1, 2, 1, 0), (3, 2, 3, 0), (0, 3, 0, 1), (1, 3, 1, 0), (3, 3, 3, 0),
    )

    def fix_sends():
        for q in (2, 1, 3):
            fix_out(q, 25 + q).start()
        for step in (1, 2, 4, 6):
            down(step).start()

    @pl.when(is_src)
    def _():
        pl.semaphore_wait(barrier, 14)

        @pl.when(k == 0)
        def _():
            @pl.when(r == 0)
            def _():
                give_fix().start()
                own_fix.start()

            for q in (0, 2, 1, 3):
                give(1, q).start()

            @pl.when(r == 0)
            def _():
                own_fix.wait()
                fix_sends()

            for slot, (q, t, x2, z2) in enumerate(plan):
                src_piece(s_hbm, q, t, slot, chip(x2, z2)).start()

            own_copy.start()
            for q in range(4):
                give(0, q).start()

        @pl.when(k == 1)
        def _():
            @pl.when(r == 0)
            def _():
                remote(
                    pf.at[fix_place(1)], pf.at[fix_place(1)], src_send.at[24], src_recv.at[4], sibling
                ).wait_recv()
                fix_sends()

            ready = []
            for slot, (q, t, x2, z2) in enumerate(plan):
                if t not in ready:
                    ready.append(t)
                    remote(
                        pf.at[line_place(1, t)], pf.at[line_place(1, t)],
                        src_send.at[16 + t], src_recv.at[t], sibling,
                    ).wait_recv()
                src_piece(pf, q, t, slot, chip(x2, z2)).start()

    loads[0].wait()
    lane = lax.broadcasted_iota(jnp.int32, (panel, 128), 1)
    for t in range(panel // 128):
        wide_line = jnp.broadcast_to(piv_ref[:, t * 128 : (t + 1) * 128], (128, 128))
        pcol[t * 128 : (t + 1) * 128, :] = jnp.transpose(wide_line)
    named = pcol[...]

    def build(t, carry):
        hit = named == lane + (r * rows + t * 128)
        oh[:, pl.ds(pl.multiple_of(t * 128, 128), 128)] = jnp.where(hit, 1.0, 0.0).astype(jnp.bfloat16)
        return carry

    lax.fori_loop(0, rows // 128, build, 0)

    def owner_of(start, size):
        return pcol[pl.ds(start, size), :] // rows

    def wide(mask_value, width):
        return jnp.concatenate([mask_value] * (width // 128), axis=1)

    width = s_ref.shape[1] // CHUNKS

    def columns(ch):
        return pl.ds(ch * width, width)

    def pick(ch):
        def body(t, carry):
            start = pl.multiple_of(t * 256, 256)
            picked = dot(oh[pl.ds(start, 256), :], s_ref[:, columns(ch)])
            owner = wide(owner_of(start, 256), width)
            old = s_ref[pl.ds(start, 256), columns(ch)].astype(jnp.float32)
            use = (owner * jnp.where(r == 0, 1, 0)) == 0
            g[pl.ds(start, 256), columns(ch)] = jnp.where(use, picked, old).astype(jnp.bfloat16)
            return carry

        lax.fori_loop(0, panel // 256, body, 0)

    def one(d, ch):
        y2 = (y + d) % NY
        return remote(
            g.at[pl.ds(pl.multiple_of(y2 * part, part), part), columns(ch)], r1.at[d - 1, :, columns(ch)],
            row_send.at[7 * ch + d - 1], row_recv.at[7 * ch + d - 1], along(y2, h),
        )

    def two(ch):
        return remote(
            zs.at[:, columns(ch)], r2.at[:, columns(ch)],
            row_send.at[7 * ch + 3], row_recv.at[7 * ch + 3], along(y, 1 - h),
        )

    def three(d, ch):
        return remote(
            msg.at[d - 1, :, columns(ch)], xf.at[pl.ds(pl.multiple_of(y * part, part), part), columns(ch)],
            row_send.at[7 * ch + 3 + d], row_recv.at[7 * ch + 3 + d], along((y + d) % NY, h),
        )

    def three_in(d, ch):
        return remote(
            msg.at[d - 1, :, columns(ch)],
            xf.at[pl.ds(pl.multiple_of(((y + NY - d) % NY) * part, part), part), columns(ch)],
            row_send.at[7 * ch + 3 + d], row_recv.at[7 * ch + 3 + d], along((y + d) % NY, h),
        )

    loads[1].wait()
    pick(0)

    @pl.when(jnp.logical_not(is_src))
    def _():
        pl.semaphore_wait(barrier, 14)

    for ch in range(CHUNKS):
        if ch:
            pick(ch)
        for d in (2, 1, 3):
            one(d, ch).start()

    def goes_x(leap, t):
        if leap == 1:
            return (z > 0) | (x == 1) | ((x == 2) & (t < 2))
        if leap == 3:
            return (z > 0) | (x == 2) | (x == 3)
        return z > 0

    def own(t, carry):
        arrived(x, t)

        @pl.when(first_plane & (x == 3) & (t < 2))
        def _():
            arrived(2, t + 2)
            net(2, t + 2, 38 + t, chip(2, 0)).start()

        @pl.when(z < NZ - 1)
        def _():
            net(x, t, t, chip(x, z + 1)).start()

        for leap in (2, 1, 3):
            @pl.when(goes_x(leap, t))
            def _():
                net(x, t, 5 * leap + t, chip((x + leap) % NX, z)).start()

        return carry

    def own_line(low, high):
        @pl.when(jnp.logical_not(is_src))
        def _():
            lax.fori_loop(low, high, own, 0)

    def own_fix_line():
        arrived(x, FIX)

        @pl.when(first_plane & (h == 0))
        def _():
            down(r + 1).start()

        @pl.when(first_plane)
        def _():
            for step in (3, 2, 1):
                net(x, FIX, (4, 40, 41)[step - 1], chip(x, step)).start()

        for leap in (2, 1, 3):
            net(x, FIX, 5 * leap + FIX, chip((x + leap) % NX, z)).start()

    def goes_back(q):
        return (z == 1) & (((x > 0) & (q == 0)) | ((x == 1) & (q == 3)) | ((x == 3) & (q == 1)))

    def relayed(q, t):
        return first_plane & (x == 3) & (q == 2) & (t >= 2)

    def others(t, carry):
        for leap in (2, 1, 3):
            q = (x + leap) % NX

            @pl.when(jnp.logical_not(relayed(q, t)))
            def _():
                arrived(q, t)

            @pl.when(goes_back(q))
            def _():
                net(q, t, 15 + 5 * leap + t, chip(x, 0)).start()

        return carry

    def other_lines(low, high):
        lax.fori_loop(low, high, others, 0)

    @pl.when(first_plane & (x > 0) & (r == 0))
    def _():
        arrived(x, FIX)
        for step in (1, 2, 4, 6):
            down(step).start()

    own_line(0, jnp.where(z == 0, 4, jnp.where(z == 1, 1, 0)))

    @pl.when(first_plane & (r > 0))
    def _():
        own_fix_line()

    home = pl.ds(pl.multiple_of(y * part, part), part)
    home_owner = wide(owner_of(pl.multiple_of(y * part, part), part), width)

    def halves(ch):
        first = jnp.zeros((part, width), jnp.float32)
        rest = jnp.zeros((part, width), jnp.float32)
        for d in range(NY):
            got = (g[home, columns(ch)] if d == 0 else r1[d - 1, :, columns(ch)]).astype(jnp.float32)
            flag = jnp.where(((y + NY - d) % NY == 0) & (h == 0), 1.0, 0.0)
            first = first + got * flag
            rest = rest + got * (1.0 - flag)
        return first, rest

    low = jnp.where(h == 0, 1, 0)
    for ch in range(CHUNKS):
        for d in (1, 3, 2):
            one(d, ch).wait_recv()
        first, rest = halves(ch)
        away = (home_owner % 2 == 0) & (home_owner != 0)
        sent_rows = jnp.where(away | (home_owner * low != home_owner), rest, jnp.where(low == 1, first, rest))
        zs[:, columns(ch)] = sent_rows.astype(jnp.bfloat16)
        two(ch).start()

    for load in loads[2:]:
        load.wait()

    def inverses():
        ub = balanced(uinv[...].astype(jnp.float32)).astype(jnp.bfloat16)
        lb = balanced(linv[...].astype(jnp.float32)).astype(jnp.bfloat16)
        both[...] = balanced(dot(ub, lb)).astype(jnp.bfloat16)

    pl.when(z != 1)(inverses)

    own_line(
        jnp.where(z == 0, 4, jnp.where(z == 1, 1, 0)),
        jnp.where(z < 3, 4, 2),
    )

    @pl.when(z == 1)
    def _():
        pl.when(r > 0)(own_fix_line)
        other_lines(0, 2)
        core_line(0).start()
        core_line(1).start()

    for ch in range(CHUNKS):
        two(ch).wait_recv()
        first, rest = halves(ch)
        got = r2[:, columns(ch)].astype(jnp.float32)
        odd = home_owner % 2 == 1
        low_t = jnp.where(odd, got, jnp.where(home_owner == 0, first, rest))
        high_t = jnp.where(odd, rest, got)
        flag = jnp.where(h == 0, 1.0, 0.0)
        new = low_t * flag + high_t * (1.0 - flag)
        old = first * flag + got * (1.0 - flag)
        for d in (2, 1, 3):
            y2 = (y + d) % NY
            msg[d - 1, :, columns(ch)] = jnp.where(home_owner == y2 * 2 + h, old, new).astype(jnp.bfloat16)
            three(d, ch).start()
        xf[home, columns(ch)] = jnp.where(home_owner == r, old, new).astype(jnp.bfloat16)

    own_line(jnp.where(z < 3, 4, 2), 4)

    @pl.when((z >= 2) & (r > 0))
    def _():
        own_fix_line()

    @pl.when(z == 1)
    def _():
        other_lines(2, 4)
        core_line(2).start()
        core_line(3).start()
        inverses()

    @pl.when(r > 0)
    def _():
        for leap in (2, 1, 3):
            arrived((x + leap) % NX, FIX)
        core_fix().start()

    bf = jnp.bfloat16
    keep = jnp.where(c == 0, 0.0, 1.0)
    left = balanced(uinv[...].astype(jnp.float32))
    for ch in range(CHUNKS):
        for d in (1, 3, 2):
            three_in(d, ch).wait_recv()

        def finish(t, carry):
            start = pl.multiple_of(t * 128, 128)
            owner = wide(owner_of(start, 128), width)
            mine = g[pl.ds(start, 128), columns(ch)].astype(jnp.float32)
            got = xf[pl.ds(start, 128), columns(ch)].astype(jnp.float32)
            tt[pl.ds(start, 128), columns(ch)] = jnp.where(owner == r, mine, got).astype(bf)
            return carry

        lax.fori_loop(0, panel // 128, finish, 0)
        right = -balanced(dot(both[...], tt[:, columns(ch)]))
        wk[:, columns(ch)] = jnp.where(c == 0, left[:, ch * width : (ch + 1) * width], right).astype(bf)

    @pl.when(r == 0)
    def _():
        xf[...] = s_ref[0:panel, :]
        lb = balanced(linv[...].astype(jnp.float32)).astype(bf)
        upper = residue(dot(lb, tt[...]))
        out[0:panel, :] = jnp.where(c == 0, tt[...].astype(jnp.float32), upper).astype(bf)

    def swapped_in(start):
        old = xf[...].astype(jnp.float32) * keep
        rep[:, 0:panel] = residue(old + dot(pf[start : start + panel, :], wk[...])).astype(bf)
        rep[:, panel : panel + 128] = jnp.ones((panel, 128), bf)

    @pl.when(r > 0)
    def _():
        core_fix_in().wait_recv()
        swapped_in(rows)

    def write(start):
        at = pl.ds(pl.multiple_of(start, panel), panel)
        return pltpu.make_async_copy(out.at[at], o_hbm.at[at], out_sem.at[start // panel])

    def tile(start):
        at = pl.ds(pl.multiple_of(start, panel), panel)

        @pl.when((r > 0) | (start >= panel))
        def _():
            index = lax.broadcasted_iota(jnp.int32, (panel, panel), 0) + (r * rows + start)
            hit = jnp.where(index == piv_ref[...], 1.0, 0.0).astype(bf)
            swapped = dot(hit, rep[...])
            count = wide(swapped[:, panel : panel + 128], panel)
            rest = residue(s_ref[at, :].astype(jnp.float32) * keep + dot(pf[at, :], wk[...]))
            out[at, :] = jnp.where(count > 0, swapped[:, 0:panel], rest).astype(bf)

        write(start).start()

    @pl.when(is_src & (k == 0))
    def _():
        own_copy.wait()

    for i in range(2):
        @pl.when((z != 1) & jnp.logical_not(is_src))
        def _():
            other_lines(2 * i, 2 * i + 2)
            core_line(2 * i).start()
            core_line(2 * i + 1).start()

        def incoming():
            core_line_in(2 * i).wait_recv()
            core_line_in(2 * i + 1).wait_recv()

        from_sibling = jnp.logical_not(is_src & (k == 0))
        if i == 0:
            @pl.when(r == 0)
            def _():
                pl.when(k == 1)(incoming)
                swapped_in(0)

            from_sibling = from_sibling & ((r > 0) | (k == 0))

        def tiles(j, carry):
            @pl.when((j == 1) & from_sibling)
            def _():
                incoming()

            tile(jnp.where(j == 0, k, 1 - k) * half + i * panel)
            return carry

        lax.fori_loop(0, 2, tiles, 0)

    for t in range(4):
        write(t * panel).wait()

    for ch in range(CHUNKS):
        for d in (1, 2, 3):
            one(d, ch).wait_send()
            three(d, ch).wait_send()
        two(ch).wait_send()
    pl.when(r > 0)(lambda: core_fix().wait_send())

    @pl.when(jnp.logical_not(is_src))
    def _():
        for q in range(4):
            core_line(q).wait_send()

        def own_sent(t, carry):
            pl.when(z < NZ - 1)(lambda: sent(t))
            for leap in range(1, 4):
                pl.when(goes_x(leap, t))(lambda: sent(5 * leap + t))
            return carry

        lax.fori_loop(0, 4, own_sent, 0)

    @pl.when(first_plane & (r > 0))
    def _():
        for slot in (4, 40, 41):
            sent(slot)

    for leap in range(1, 4):
        pl.when(r > 0)(lambda: sent(5 * leap + FIX))

        @pl.when(goes_back((x + leap) % NX))
        def _():
            for t in range(4):
                sent(15 + 5 * leap + t)

    @pl.when(first_plane & (x == 3))
    def _():
        sent(38)
        sent(39)

    @pl.when(is_src)
    def _():
        for slot, (q, t, x2, z2) in enumerate(plan):
            src_piece(pf, q, t, slot, chip(x2, z2)).wait_send()

        @pl.when(r == 0)
        def _():
            for q in (2, 1, 3):
                fix_out(q, 25 + q).wait_send()

        @pl.when(k == 0)
        def _():
            for q in range(4):
                give(1, q).wait_send()
                give(0, q).wait_send()

            @pl.when(r == 0)
            def _():
                give_fix().wait_send()

    @pl.when(first_plane & (r == 0))
    def _():
        for step in (1, 2, 4, 6):
            down(step).wait_send()

    @pl.when(first_plane & (r > 0) & (h == 0))
    def _():
        down(r + 1).wait_send()


def step_kernel(piv, linv, uinv, s, panel):
    rows, cols = s.shape
    part = panel // NY
    bf = jnp.bfloat16
    dma = pltpu.SemaphoreType.DMA
    anywhere = pl.BlockSpec(memory_space=pl.ANY)
    return pl.pallas_call(
        exchange_kernel,
        out_shape=jax.ShapeDtypeStruct((rows, cols), bf),
        in_specs=[pl.BlockSpec(memory_space=pltpu.HBM)] * 4,
        out_specs=anywhere,
        scratch_shapes=[
            pltpu.VMEM((1, panel), jnp.int32),
            pltpu.VMEM((panel, panel), bf),
            pltpu.VMEM((panel, panel), bf),
            pltpu.VMEM((rows, cols), bf),
            pltpu.VMEM((rows + panel, panel), bf),
            pltpu.VMEM((panel, cols), bf),
            pltpu.VMEM((panel, cols), bf),
            pltpu.VMEM((panel, panel), bf),
            pltpu.VMEM((panel, cols), bf),
            pltpu.VMEM((panel, cols + 128), bf),
            pltpu.VMEM((rows, cols), bf),
            pltpu.VMEM((panel, 128), jnp.int32),
            pltpu.VMEM((panel, rows), bf),
            pltpu.VMEM((panel, cols), bf),
            pltpu.VMEM((NY - 1, part, cols), bf),
            pltpu.VMEM((part, cols), bf),
            pltpu.VMEM((part, cols), bf),
            pltpu.VMEM((NY - 1, part, cols), bf),
            dma((42,)), dma((20,)), dma((29,)), dma((5,)), dma((5,)), dma((5,)),
            dma((7,)), dma((7 * CHUNKS,)), dma((7 * CHUNKS,)), dma((6,)), dma((4,)),
        ],
        compiler_params=pltpu.CompilerParams(
            collective_id=0, has_side_effects=True, vmem_limit_bytes=60 << 20
        ),
        name="exchange",
    )(piv, linv, uinv, s)


def per_device(matrix, pivots, lower_inverse, upper_inverse):
    panel = lower_inverse.shape[0]
    piv = pivots.reshape(1, panel)
    rest = step_kernel(piv, lower_inverse, upper_inverse, matrix, panel)
    return rest.astype(jnp.float32) * INVERSE


def solution(mesh):
    placed = (P("row", "col"), P(), P(), P())
    return jax.shard_map(
        per_device, mesh=mesh, in_specs=placed, out_specs=P("row", "col"), check_vma=False
    )
```

```python
import functools

import jax
import jax.numpy as jnp
from jax import lax
from jax.experimental import pallas as pl
from jax.experimental.pallas import tpu as pltpu
from jax.sharding import PartitionSpec as P

MESH = pl.DeviceIdType.MESH
PRIME = 251.0
INVERSE = 1.0 / 251.0
ROUND = 1.5 * 2.0**23
NY, NX, NZ = 4, 4, 4
CHUNKS = 2
FIX = 4


def balanced(x):
    quot = (x * INVERSE + ROUND) - ROUND
    return x - quot * PRIME


def residue(x):
    rest = balanced(x)
    return jnp.where(rest < 0, rest + PRIME, rest)


def dot(a, b):
    return jnp.dot(a, b, preferred_element_type=jnp.float32)


def exchange_kernel(
    piv_hbm, linv_hbm, uinv_hbm, s_hbm, o_hbm, piv_ref, linv, uinv, out, pf, tt, xf, both, wk, rep, s_ref, pcol, oh, g, r1, zs, r2, msg,
    net_send, net_recv, src_send, src_recv, core_send, core_recv, down_send, row_send, row_recv, loc, out_sem,
):
    rows = s_ref.shape[0]
    panel = xf.shape[0]
    half = rows // 2
    line = half // NX
    piece = line // 4
    fix = panel // 2
    part = panel // NY
    r = lax.axis_index("row")
    c = lax.axis_index("col")
    y, h = r // 2, r % 2
    x, z, k = c // 8, (c // 2) % 4, c % 2
    first_plane = z == 0
    is_src = first_plane & (x == 0)
    quarter = rows // 4
    spans = [pl.ds(i * quarter, quarter) for i in range(4)]
    pairs = [(piv_hbm, piv_ref)]
    pairs += [(s_hbm.at[at], s_ref.at[at]) for at in spans]
    pairs += [(uinv_hbm, uinv), (linv_hbm, linv)]
    loads = [
        pltpu.make_async_copy(src, dst, loc.at[2 + i]) for i, (src, dst) in enumerate(pairs)
    ]
    for load in loads:
        load.start()

    def chip(x2, z2):
        return {"row": r, "col": x2 * 8 + z2 * 2 + k}

    def along(y2, h2):
        return {"row": y2 * 2 + h2, "col": c}

    sibling = {"row": r, "col": c + 1 - 2 * k}
    barrier = pltpu.get_barrier_semaphore()

    def signal(device):
        pl.semaphore_signal(barrier, 1, device_id=device, device_id_type=MESH)

    signal(sibling)
    for step in range(1, 4):
        signal(chip((x + step) % NX, z))
        signal(chip(x, (z + step) % NZ))
    for step in range(1, 8):
        signal({"row": (r + step) % 8, "col": c})

    def remote(src, dst, send, recv, device):
        return pltpu.make_async_remote_copy(
            src_ref=src, dst_ref=dst, send_sem=send, recv_sem=recv,
            device_id=device, device_id_type=MESH,
        )

    def place(q, t):
        if isinstance(t, int) and t == FIX:
            return pl.ds(pl.multiple_of(rows + k * fix + q * piece, piece), piece)
        return pl.ds(pl.multiple_of(k * half + t * line + q * piece, piece), piece)

    def net(q, t, slot, device):
        return remote(
            pf.at[place(q, t)], pf.at[place(q, t)], net_send.at[slot], net_recv.at[q * 5 + t], device
        )

    def arrived(q, t):
        net(q, t, 0, sibling).wait_recv()

    def sent(slot):
        net(0, 0, slot, sibling).wait_send()

    def src_piece(ref, q, t, slot, device):
        return remote(
            ref.at[place(q, t)], pf.at[place(q, t)], src_send.at[slot], net_recv.at[q * 5 + t], device
        )

    def line_place(k2, q):
        return pl.ds(pl.multiple_of(k2 * half + q * line, line), line)

    def core_line(q):
        return remote(
            pf.at[line_place(k, q)], pf.at[line_place(k, q)], core_send.at[q], core_recv.at[q], sibling
        )

    def core_line_in(q):
        return remote(
            pf.at[line_place(1 - k, q)], pf.at[line_place(1 - k, q)],
            core_send.at[q], core_recv.at[q], sibling,
        )

    def fix_place(k2):
        return pl.ds(pl.multiple_of(rows + k2 * fix, fix), fix)

    def core_fix():
        return remote(
            pf.at[fix_place(k)], pf.at[fix_place(k)], core_send.at[4], core_recv.at[4], sibling
        )

    def core_fix_in():
        return remote(
            pf.at[fix_place(1 - k)], pf.at[fix_place(1 - k)],
            core_send.at[4], core_recv.at[4], sibling,
        )

    def give(k2, q):
        at = pl.ds(k2 * half + q * line, line)
        return remote(
            s_hbm.at[at], pf.at[at], src_send.at[28 + k2 * 4 + q],
            src_recv.at[q] if k2 else core_recv.at[q], sibling,
        )

    def give_fix():
        return remote(
            s_hbm.at[pl.ds(fix, fix)], pf.at[pl.ds(rows + fix, fix)],
            src_send.at[36], src_recv.at[4], sibling,
        )

    own_copy = pltpu.make_async_copy(s_hbm, pf.at[pl.ds(0, rows)], loc.at[0])
    own_fix = pltpu.make_async_copy(s_hbm.at[pl.ds(0, fix)], pf.at[pl.ds(rows, fix)], loc.at[1])

    def fix_out(q, slot):
        return remote(
            pf.at[place(q, 4)], pf.at[place(q, 4)], src_send.at[slot], net_recv.at[q * 5 + 4], chip(q, 0)
        )

    def down(step):
        return remote(
            pf.at[place(x, FIX)], pf.at[place(x, FIX)], down_send.at[step // 2 if isinstance(step, int) else 0],
            net_recv.at[x * 5 + FIX], {"row": step, "col": c},
        )

    plan = (
        (2, 0, 2, 0), (3, 0, 3, 0), (0, 0, 0, 1), (1, 0, 1, 0), (2, 2, 3, 0), (0, 1, 0, 1),
        (2, 1, 2, 0), (3, 1, 3, 0), (1, 1, 1, 0), (2, 3, 3, 0), (0, 2, 0, 1),
        (1, 2, 1, 0), (3, 2, 3, 0), (0, 3, 0, 1), (1, 3, 1, 0), (3, 3, 3, 0),
    ) + tuple((0, t, x2, 0) for t in range(4) for x2 in (1, 3, 2))

    def fix_sends():
        for q in (2, 1, 3):
            fix_out(q, 36 + q).start()
        for step in (1, 2, 4, 6):
            down(step).start()

    @pl.when(is_src)
    def _():
        pl.semaphore_wait(barrier, 14)

        @pl.when(k == 0)
        def _():
            @pl.when(r == 0)
            def _():
                give_fix().start()
                own_fix.start()

            for q in (0, 2, 1, 3):
                give(1, q).start()

            @pl.when(r == 0)
            def _():
                own_fix.wait()
                fix_sends()

            for slot, (q, t, x2, z2) in enumerate(plan):
                src_piece(s_hbm, q, t, slot, chip(x2, z2)).start()

            own_copy.start()
            for q in range(4):
                give(0, q).start()

        @pl.when(k == 1)
        def _():
            @pl.when(r == 0)
            def _():
                remote(
                    pf.at[fix_place(1)], pf.at[fix_place(1)], src_send.at[36], src_recv.at[4], sibling
                ).wait_recv()
                fix_sends()

            ready = []
            for slot, (q, t, x2, z2) in enumerate(plan):
                if t not in ready:
                    ready.append(t)
                    remote(
                        pf.at[line_place(1, t)], pf.at[line_place(1, t)],
                        src_send.at[28 + t], src_recv.at[t], sibling,
                    ).wait_recv()
                src_piece(pf, q, t, slot, chip(x2, z2)).start()

    loads[0].wait()
    lane = lax.broadcasted_iota(jnp.int32, (panel, 128), 1)
    for t in range(panel // 128):
        wide_line = jnp.broadcast_to(piv_ref[:, t * 128 : (t + 1) * 128], (128, 128))
        pcol[t * 128 : (t + 1) * 128, :] = jnp.transpose(wide_line)
    named = pcol[...]

    def build(t, carry):
        hit = named == lane + (r * rows + t * 128)
        oh[:, pl.ds(pl.multiple_of(t * 128, 128), 128)] = jnp.where(hit, 1.0, 0.0).astype(jnp.bfloat16)
        return carry

    lax.fori_loop(0, rows // 128, build, 0)

    def owner_of(start, size):
        return pcol[pl.ds(start, size), :] // rows

    def wide(mask_value, width):
        return jnp.concatenate([mask_value] * (width // 128), axis=1)

    width = s_ref.shape[1] // CHUNKS

    def columns(ch):
        return pl.ds(ch * width, width)

    def pick(ch):
        def body(t, carry):
            start = pl.multiple_of(t * 256, 256)
            picked = dot(oh[pl.ds(start, 256), :], s_ref[:, columns(ch)])
            owner = wide(owner_of(start, 256), width)
            old = s_ref[pl.ds(start, 256), columns(ch)].astype(jnp.float32)
            use = (owner * jnp.where(r == 0, 1, 0)) == 0
            g[pl.ds(start, 256), columns(ch)] = jnp.where(use, picked, old).astype(jnp.bfloat16)
            return carry

        lax.fori_loop(0, panel // 256, body, 0)

    def one(d, ch):
        y2 = (y + d) % NY
        return remote(
            g.at[pl.ds(pl.multiple_of(y2 * part, part), part), columns(ch)], r1.at[d - 1, :, columns(ch)],
            row_send.at[7 * ch + d - 1], row_recv.at[7 * ch + d - 1], along(y2, h),
        )

    def two(ch):
        return remote(
            zs.at[:, columns(ch)], r2.at[:, columns(ch)],
            row_send.at[7 * ch + 3], row_recv.at[7 * ch + 3], along(y, 1 - h),
        )

    def three(d, ch):
        return remote(
            msg.at[d - 1, :, columns(ch)], xf.at[pl.ds(pl.multiple_of(y * part, part), part), columns(ch)],
            row_send.at[7 * ch + 3 + d], row_recv.at[7 * ch + 3 + d], along((y + d) % NY, h),
        )

    def three_in(d, ch):
        return remote(
            msg.at[d - 1, :, columns(ch)],
            xf.at[pl.ds(pl.multiple_of(((y + NY - d) % NY) * part, part), part), columns(ch)],
            row_send.at[7 * ch + 3 + d], row_recv.at[7 * ch + 3 + d], along((y + d) % NY, h),
        )

    for load in loads[1:5]:
        load.wait()
    pick(0)

    @pl.when(jnp.logical_not(is_src))
    def _():
        pl.semaphore_wait(barrier, 14)

    for ch in range(CHUNKS):
        if ch:
            pick(ch)
        for d in (2, 1, 3):
            one(d, ch).start()
        if ch == 0:
            @pl.when(first_plane & (x > 0) & (r == 0))
            def _():
                arrived(x, FIX)
                for step in (1, 2, 4, 6):
                    down(step).start()

    def goes_x(leap, t):
        return (z > 0) | (((x + leap) % NX != 0) & ((x != 2) | (leap != 1) | (t < 2)))

    def along_x(t, carry):
        for leap in (1, 3, 2):
            @pl.when(goes_x(leap, t))
            def _():
                net(x, t, 5 * leap + t, chip((x + leap) % NX, z)).start()

        return carry

    def own(t, carry):
        arrived(x, t)

        @pl.when(first_plane & (x == 3) & (t < 2))
        def _():
            arrived(2, t + 2)
            net(2, t + 2, 38 + t, chip(2, 0)).start()

        @pl.when(z < NZ - 1)
        def _():
            net(x, t, t, chip(x, z + 1)).start()

        @pl.when(z > 0)
        def _():
            along_x(t, 0)

        return carry

    def own_line(low, high):
        @pl.when(jnp.logical_not(is_src))
        def _():
            lax.fori_loop(low, high, own, 0)

    def own_fix_line():
        arrived(x, FIX)

        @pl.when(first_plane & (h == 0))
        def _():
            down(r + 1).start()

        @pl.when(first_plane)
        def _():
            for step in (3, 2, 1):
                net(x, FIX, (4, 40, 41)[step - 1], chip(x, step)).start()

        for leap in (2, 1, 3):
            net(x, FIX, 5 * leap + FIX, chip((x + leap) % NX, z)).start()

    def relayed(q, t):
        return first_plane & (x == 3) & (q == 2) & (t >= 2)

    def others(t, carry):
        for leap in (2, 1, 3):
            q = (x + leap) % NX

            @pl.when(jnp.logical_not(relayed(q, t)))
            def _():
                arrived(q, t)

        return carry

    def other_lines(low, high):
        lax.fori_loop(low, high, others, 0)

    early = (r == 1) | ((h == 0) & (r > 0))
    late = (h == 1) & (r > 1)
    own_line(0, jnp.where(z == 0, jnp.where(early, 2, 4), jnp.where(z == 1, 1, 0)))
    pl.when(first_plane & early)(own_fix_line)
    own_line(jnp.where(first_plane & early, 2, 4), 4)

    home = pl.ds(pl.multiple_of(y * part, part), part)
    home_owner = wide(owner_of(pl.multiple_of(y * part, part), part), width)

    def halves(ch):
        first = jnp.zeros((part, width), jnp.float32)
        rest = jnp.zeros((part, width), jnp.float32)
        for d in range(NY):
            got = (g[home, columns(ch)] if d == 0 else r1[d - 1, :, columns(ch)]).astype(jnp.float32)
            flag = jnp.where(((y + NY - d) % NY == 0) & (h == 0), 1.0, 0.0)
            first = first + got * flag
            rest = rest + got * (1.0 - flag)
        return first, rest

    low = jnp.where(h == 0, 1, 0)
    for ch in range(CHUNKS):
        for d in (1, 3, 2):
            one(d, ch).wait_recv()
        first, rest = halves(ch)
        away = (home_owner % 2 == 0) & (home_owner != 0)
        sent_rows = jnp.where(away | (home_owner * low != home_owner), rest, jnp.where(low == 1, first, rest))
        zs[:, columns(ch)] = sent_rows.astype(jnp.bfloat16)
        two(ch).start()

    for load in loads[5:]:
        load.wait()

    def inverses():
        ub = balanced(uinv[...].astype(jnp.float32)).astype(jnp.bfloat16)
        lb = balanced(linv[...].astype(jnp.float32)).astype(jnp.bfloat16)
        both[...] = balanced(dot(ub, lb)).astype(jnp.bfloat16)

    pl.when(first_plane & late)(own_fix_line)

    @pl.when(first_plane & (x > 0))
    def _():
        lax.fori_loop(0, 4, along_x, 0)

    inverses()
    own_line(jnp.where(z == 0, 4, jnp.where(z == 1, 1, 0)), jnp.where(z < 2, 4, 4 - z))
    pl.when((z > 0) & (r > 0))(own_fix_line)
    own_line(jnp.where(z < 2, 4, 4 - z), jnp.where(z < 2, 4, 2))

    for ch in range(CHUNKS):
        two(ch).wait_recv()
        first, rest = halves(ch)
        got = r2[:, columns(ch)].astype(jnp.float32)
        odd = home_owner % 2 == 1
        low_t = jnp.where(odd, got, jnp.where(home_owner == 0, first, rest))
        high_t = jnp.where(odd, rest, got)
        flag = jnp.where(h == 0, 1.0, 0.0)
        new = low_t * flag + high_t * (1.0 - flag)
        old = first * flag + got * (1.0 - flag)
        for d in (2, 1, 3):
            y2 = (y + d) % NY
            msg[d - 1, :, columns(ch)] = jnp.where(home_owner == y2 * 2 + h, old, new).astype(jnp.bfloat16)
            three(d, ch).start()
        xf[home, columns(ch)] = jnp.where(home_owner == r, old, new).astype(jnp.bfloat16)

    own_line(jnp.where(z < 2, 4, 2), 4)

    @pl.when(r > 0)
    def _():
        for leap in (2, 1, 3):
            arrived((x + leap) % NX, FIX)
        core_fix().start()

    bf = jnp.bfloat16
    keep = jnp.where(c == 0, 0.0, 1.0)
    left = balanced(uinv[...].astype(jnp.float32))
    for ch in range(CHUNKS):
        for d in (1, 3, 2):
            three_in(d, ch).wait_recv()

        def finish(t, carry):
            start = pl.multiple_of(t * 128, 128)
            owner = wide(owner_of(start, 128), width)
            mine = g[pl.ds(start, 128), columns(ch)].astype(jnp.float32)
            got = xf[pl.ds(start, 128), columns(ch)].astype(jnp.float32)
            tt[pl.ds(start, 128), columns(ch)] = jnp.where(owner == r, mine, got).astype(bf)
            return carry

        lax.fori_loop(0, panel // 128, finish, 0)
        right = -balanced(dot(both[...], tt[:, columns(ch)]))
        wk[:, columns(ch)] = jnp.where(c == 0, left[:, ch * width : (ch + 1) * width], right).astype(bf)

    @pl.when(r == 0)
    def _():
        xf[...] = s_ref[0:panel, :]
        lb = balanced(linv[...].astype(jnp.float32)).astype(bf)
        upper = residue(dot(lb, tt[...]))
        out[0:panel, :] = jnp.where(c == 0, tt[...].astype(jnp.float32), upper).astype(bf)

    def swapped_in(start):
        old = xf[...].astype(jnp.float32) * keep
        rep[:, 0:panel] = residue(old + dot(pf[start : start + panel, :], wk[...])).astype(bf)
        rep[:, panel : panel + 128] = jnp.ones((panel, 128), bf)

    @pl.when(r > 0)
    def _():
        core_fix_in().wait_recv()
        swapped_in(rows)

    def write(start):
        at = pl.ds(pl.multiple_of(start, panel), panel)
        return pltpu.make_async_copy(out.at[at], o_hbm.at[at], out_sem.at[start // panel])

    def tile(start):
        at = pl.ds(pl.multiple_of(start, panel), panel)

        @pl.when((r > 0) | (start >= panel))
        def _():
            index = lax.broadcasted_iota(jnp.int32, (panel, panel), 0) + (r * rows + start)
            hit = jnp.where(index == piv_ref[...], 1.0, 0.0).astype(bf)
            swapped = dot(hit, rep[...])
            count = wide(swapped[:, panel : panel + 128], panel)
            rest = residue(s_ref[at, :].astype(jnp.float32) * keep + dot(pf[at, :], wk[...]))
            out[at, :] = jnp.where(count > 0, swapped[:, 0:panel], rest).astype(bf)

        write(start).start()

    @pl.when(is_src & (k == 0))
    def _():
        own_copy.wait()

    for i in range(2):
        @pl.when(jnp.logical_not(is_src))
        def _():
            other_lines(2 * i, 2 * i + 2)
            core_line(2 * i).start()
            core_line(2 * i + 1).start()

        def incoming():
            core_line_in(2 * i).wait_recv()
            core_line_in(2 * i + 1).wait_recv()

        from_sibling = jnp.logical_not(is_src & (k == 0))
        if i == 0:
            @pl.when(r == 0)
            def _():
                pl.when(k == 1)(incoming)
                swapped_in(0)

            from_sibling = from_sibling & ((r > 0) | (k == 0))

        def tiles(j, carry):
            @pl.when((j == 1) & from_sibling)
            def _():
                incoming()

            tile(jnp.where(j == 0, k, 1 - k) * half + i * panel)
            return carry

        lax.fori_loop(0, 2, tiles, 0)

    for t in range(4):
        write(t * panel).wait()

    for ch in range(CHUNKS):
        for d in (1, 2, 3):
            one(d, ch).wait_send()
            three(d, ch).wait_send()
        two(ch).wait_send()
    pl.when(r > 0)(lambda: core_fix().wait_send())

    @pl.when(jnp.logical_not(is_src))
    def _():
        for q in range(4):
            core_line(q).wait_send()

        def own_sent(t, carry):
            pl.when(z < NZ - 1)(lambda: sent(t))
            for leap in range(1, 4):
                pl.when(goes_x(leap, t))(lambda: sent(5 * leap + t))
            return carry

        lax.fori_loop(0, 4, own_sent, 0)

    @pl.when(first_plane & (r > 0))
    def _():
        for slot in (4, 40, 41):
            sent(slot)

    for leap in range(1, 4):
        pl.when(r > 0)(lambda: sent(5 * leap + FIX))

    @pl.when(first_plane & (x == 3))
    def _():
        sent(38)
        sent(39)

    @pl.when(is_src)
    def _():
        for slot, (q, t, x2, z2) in enumerate(plan):
            src_piece(pf, q, t, slot, chip(x2, z2)).wait_send()

        @pl.when(r == 0)
        def _():
            for q in (2, 1, 3):
                fix_out(q, 36 + q).wait_send()

        @pl.when(k == 0)
        def _():
            for q in range(4):
                give(1, q).wait_send()
                give(0, q).wait_send()

            @pl.when(r == 0)
            def _():
                give_fix().wait_send()

    @pl.when(first_plane & (r == 0))
    def _():
        for step in (1, 2, 4, 6):
            down(step).wait_send()

    @pl.when(first_plane & (r > 0) & (h == 0))
    def _():
        down(r + 1).wait_send()


def step_kernel(piv, linv, uinv, s, panel):
    rows, cols = s.shape
    part = panel // NY
    bf = jnp.bfloat16
    dma = pltpu.SemaphoreType.DMA
    anywhere = pl.BlockSpec(memory_space=pl.ANY)
    return pl.pallas_call(
        exchange_kernel,
        out_shape=jax.ShapeDtypeStruct((rows, cols), bf),
        in_specs=[pl.BlockSpec(memory_space=pltpu.HBM)] * 4,
        out_specs=anywhere,
        scratch_shapes=[
            pltpu.VMEM((1, panel), jnp.int32),
            pltpu.VMEM((panel, panel), bf),
            pltpu.VMEM((panel, panel), bf),
            pltpu.VMEM((rows, cols), bf),
            pltpu.VMEM((rows + panel, panel), bf),
            pltpu.VMEM((panel, cols), bf),
            pltpu.VMEM((panel, cols), bf),
            pltpu.VMEM((panel, panel), bf),
            pltpu.VMEM((panel, cols), bf),
            pltpu.VMEM((panel, cols + 128), bf),
            pltpu.VMEM((rows, cols), bf),
            pltpu.VMEM((panel, 128), jnp.int32),
            pltpu.VMEM((panel, rows), bf),
            pltpu.VMEM((panel, cols), bf),
            pltpu.VMEM((NY - 1, part, cols), bf),
            pltpu.VMEM((part, cols), bf),
            pltpu.VMEM((part, cols), bf),
            pltpu.VMEM((NY - 1, part, cols), bf),
            dma((42,)), dma((20,)), dma((40,)), dma((5,)), dma((5,)), dma((5,)),
            dma((7,)), dma((7 * CHUNKS,)), dma((7 * CHUNKS,)), dma((9,)), dma((4,)),
        ],
        compiler_params=pltpu.CompilerParams(
            collective_id=0, has_side_effects=True, vmem_limit_bytes=60 << 20
        ),
        name="exchange",
    )(piv, linv, uinv, s)


def divide_kernel(x_hbm, o_hbm, x, o, sem_in, sem_out):
    parts = sem_in.shape[0]
    size = x.shape[0] // parts
    spans = [pl.ds(i * size, size) for i in range(parts)]
    loads = [pltpu.make_async_copy(x_hbm.at[at], x.at[at], sem_in.at[i]) for i, at in enumerate(spans)]
    stores = [pltpu.make_async_copy(o.at[at], o_hbm.at[at], sem_out.at[i]) for i, at in enumerate(spans)]
    for load in loads:
        load.start()
    for at, load, store in zip(spans, loads, stores):
        load.wait()
        o[at, :] = x[at, :].astype(jnp.float32) * INVERSE
        store.start()
    for store in stores:
        store.wait()


def divide(x):
    anywhere = pl.BlockSpec(memory_space=pl.ANY)
    parts = 8
    return pl.pallas_call(
        divide_kernel,
        out_shape=jax.ShapeDtypeStruct(x.shape, jnp.float32),
        in_specs=[anywhere],
        out_specs=anywhere,
        scratch_shapes=[
            pltpu.VMEM(x.shape, x.dtype),
            pltpu.VMEM(x.shape, jnp.float32),
            pltpu.SemaphoreType.DMA((parts,)),
            pltpu.SemaphoreType.DMA((parts,)),
        ],
        compiler_params=pltpu.CompilerParams(vmem_limit_bytes=60 << 20),
        name="divide",
    )(x)


def per_device(matrix, pivots, lower_inverse, upper_inverse):
    panel = lower_inverse.shape[0]
    piv = pivots.reshape(1, panel)
    return divide(step_kernel(piv, lower_inverse, upper_inverse, matrix, panel))


def solution(mesh):
    placed = (P("row", "col"), P(), P(), P())
    return jax.shard_map(
        per_device, mesh=mesh, in_specs=placed, out_specs=P("row", "col"), check_vma=False
    )
```

```python
import functools

import jax
import jax.numpy as jnp
from jax import lax
from jax.experimental import pallas as pl
from jax.experimental.pallas import tpu as pltpu
from jax.sharding import PartitionSpec as P

MESH = pl.DeviceIdType.MESH
PRIME = 251.0
INVERSE = 1.0 / 251.0
ROUND = 1.5 * 2.0**23
NY, NX, NZ = 4, 4, 4
CHUNKS = 2
FIX = 4


def balanced(x):
    quot = (x * INVERSE + ROUND) - ROUND
    return x - quot * PRIME


def residue(x):
    rest = balanced(x)
    return jnp.where(rest < 0, rest + PRIME, rest)


def dot(a, b):
    return jnp.dot(a, b, preferred_element_type=jnp.float32)


def exchange_kernel(
    piv_hbm, linv_hbm, uinv_hbm, s_hbm, o_hbm, piv_ref, linv, uinv, out, pf, tt, xf, both, wk, rep, s_ref, pcol, oh, g, r1, zs, r2, msg,
    net_send, net_recv, src_send, src_recv, core_send, core_recv, down_send, row_send, row_recv, loc, out_sem,
):
    rows = s_ref.shape[0]
    panel = xf.shape[0]
    half = rows // 2
    line = half // NX
    piece = line // 4
    fix = panel // 2
    part = panel // NY
    r = lax.axis_index("row")
    c = lax.axis_index("col")
    y, h = r // 2, r % 2
    x, z, k = c // 8, (c // 2) % 4, c % 2
    first_plane = z == 0
    is_src = first_plane & (x == 0)
    quarter = rows // 4
    spans = [pl.ds(i * quarter, quarter) for i in range(4)]
    pairs = [(piv_hbm, piv_ref)]
    pairs += [(s_hbm.at[at], s_ref.at[at]) for at in spans]
    pairs += [(uinv_hbm, uinv), (linv_hbm, linv)]
    loads = [
        pltpu.make_async_copy(src, dst, loc.at[2 + i]) for i, (src, dst) in enumerate(pairs)
    ]
    for load in loads:
        load.start()

    def chip(x2, z2):
        return {"row": r, "col": x2 * 8 + z2 * 2 + k}

    def along(y2, h2):
        return {"row": y2 * 2 + h2, "col": c}

    sibling = {"row": r, "col": c + 1 - 2 * k}
    barrier = pltpu.get_barrier_semaphore()

    def signal(device):
        pl.semaphore_signal(barrier, 1, device_id=device, device_id_type=MESH)

    signal(sibling)
    for step in range(1, 4):
        signal(chip((x + step) % NX, z))
        signal(chip(x, (z + step) % NZ))
    for step in range(1, 8):
        signal({"row": (r + step) % 8, "col": c})

    def remote(src, dst, send, recv, device):
        return pltpu.make_async_remote_copy(
            src_ref=src, dst_ref=dst, send_sem=send, recv_sem=recv,
            device_id=device, device_id_type=MESH,
        )

    def place(q, t):
        if isinstance(t, int) and t == FIX:
            return pl.ds(pl.multiple_of(rows + k * fix + q * piece, piece), piece)
        return pl.ds(pl.multiple_of(k * half + t * line + q * piece, piece), piece)

    def net(q, t, slot, device):
        return remote(
            pf.at[place(q, t)], pf.at[place(q, t)], net_send.at[slot], net_recv.at[q * 5 + t], device
        )

    def arrived(q, t):
        net(q, t, 0, sibling).wait_recv()

    def sent(slot):
        net(0, 0, slot, sibling).wait_send()

    def src_piece(ref, q, t, slot, device):
        return remote(
            ref.at[place(q, t)], pf.at[place(q, t)], src_send.at[slot], net_recv.at[q * 5 + t], device
        )

    def line_place(k2, q):
        return pl.ds(pl.multiple_of(k2 * half + q * line, line), line)

    def core_line(q):
        return remote(
            pf.at[line_place(k, q)], pf.at[line_place(k, q)], core_send.at[q], core_recv.at[q], sibling
        )

    def core_line_in(q):
        return remote(
            pf.at[line_place(1 - k, q)], pf.at[line_place(1 - k, q)],
            core_send.at[q], core_recv.at[q], sibling,
        )

    def fix_place(k2):
        return pl.ds(pl.multiple_of(rows + k2 * fix, fix), fix)

    def core_fix():
        return remote(
            pf.at[fix_place(k)], pf.at[fix_place(k)], core_send.at[4], core_recv.at[4], sibling
        )

    def core_fix_in():
        return remote(
            pf.at[fix_place(1 - k)], pf.at[fix_place(1 - k)],
            core_send.at[4], core_recv.at[4], sibling,
        )

    def give(k2, q):
        at = pl.ds(k2 * half + q * line, line)
        return remote(
            s_hbm.at[at], pf.at[at], src_send.at[28 + k2 * 4 + q],
            src_recv.at[q] if k2 else core_recv.at[q], sibling,
        )

    def give_fix():
        return remote(
            s_hbm.at[pl.ds(fix, fix)], pf.at[pl.ds(rows + fix, fix)],
            src_send.at[36], src_recv.at[4], sibling,
        )

    own_copy = pltpu.make_async_copy(s_hbm, pf.at[pl.ds(0, rows)], loc.at[0])
    own_fix = pltpu.make_async_copy(s_hbm.at[pl.ds(0, fix)], pf.at[pl.ds(rows, fix)], loc.at[1])

    def fix_out(q, slot):
        return remote(
            pf.at[place(q, 4)], pf.at[place(q, 4)], src_send.at[slot], net_recv.at[q * 5 + 4], chip(q, 0)
        )

    def down(step):
        return remote(
            pf.at[place(x, FIX)], pf.at[place(x, FIX)], down_send.at[step // 2 if isinstance(step, int) else 0],
            net_recv.at[x * 5 + FIX], {"row": step, "col": c},
        )

    plan = (
        (2, 0, 2, 0), (3, 0, 3, 0), (0, 0, 0, 1), (1, 0, 1, 0), (2, 2, 3, 0), (0, 1, 0, 1),
        (2, 1, 2, 0), (3, 1, 3, 0), (1, 1, 1, 0), (2, 3, 3, 0), (0, 2, 0, 1),
        (1, 2, 1, 0), (3, 2, 3, 0), (0, 3, 0, 1), (1, 3, 1, 0), (3, 3, 3, 0),
    ) + tuple((0, t, x2, 0) for t in range(4) for x2 in (1, 3, 2))

    def fix_sends():
        for q in (2, 1, 3):
            fix_out(q, 36 + q).start()
        for step in (1, 2, 4, 6):
            down(step).start()

    @pl.when(is_src)
    def _():
        pl.semaphore_wait(barrier, 14)

        @pl.when(k == 0)
        def _():
            @pl.when(r == 0)
            def _():
                give_fix().start()
                own_fix.start()

            for q in (0, 2, 1, 3):
                give(1, q).start()

            @pl.when(r == 0)
            def _():
                own_fix.wait()
                fix_sends()

            for slot, (q, t, x2, z2) in enumerate(plan):
                src_piece(s_hbm, q, t, slot, chip(x2, z2)).start()

            own_copy.start()
            for q in range(4):
                give(0, q).start()

        @pl.when(k == 1)
        def _():
            @pl.when(r == 0)
            def _():
                remote(
                    pf.at[fix_place(1)], pf.at[fix_place(1)], src_send.at[36], src_recv.at[4], sibling
                ).wait_recv()
                fix_sends()

            ready = []
            for slot, (q, t, x2, z2) in enumerate(plan):
                if t not in ready:
                    ready.append(t)
                    remote(
                        pf.at[line_place(1, t)], pf.at[line_place(1, t)],
                        src_send.at[28 + t], src_recv.at[t], sibling,
                    ).wait_recv()
                src_piece(pf, q, t, slot, chip(x2, z2)).start()

    loads[0].wait()
    lane = lax.broadcasted_iota(jnp.int32, (panel, 128), 1)
    for t in range(panel // 128):
        wide_line = jnp.broadcast_to(piv_ref[:, t * 128 : (t + 1) * 128], (128, 128))
        pcol[t * 128 : (t + 1) * 128, :] = jnp.transpose(wide_line)
    named = pcol[...]

    def build(t, carry):
        hit = named == lane + (r * rows + t * 128)
        oh[:, pl.ds(pl.multiple_of(t * 128, 128), 128)] = jnp.where(hit, 1.0, 0.0).astype(jnp.bfloat16)
        return carry

    lax.fori_loop(0, rows // 128, build, 0)

    def owner_of(start, size):
        return pcol[pl.ds(start, size), :] // rows

    def wide(mask_value, width):
        return jnp.concatenate([mask_value] * (width // 128), axis=1)

    width = s_ref.shape[1] // CHUNKS

    def columns(ch):
        return pl.ds(ch * width, width)

    def pick(ch):
        def body(t, carry):
            start = pl.multiple_of(t * 256, 256)
            picked = dot(oh[pl.ds(start, 256), :], s_ref[:, columns(ch)])
            owner = wide(owner_of(start, 256), width)
            old = s_ref[pl.ds(start, 256), columns(ch)].astype(jnp.float32)
            use = (owner * jnp.where(r == 0, 1, 0)) == 0
            g[pl.ds(start, 256), columns(ch)] = jnp.where(use, picked, old).astype(jnp.bfloat16)
            return carry

        lax.fori_loop(0, panel // 256, body, 0)

    def one(d, ch):
        y2 = (y + d) % NY
        return remote(
            g.at[pl.ds(pl.multiple_of(y2 * part, part), part), columns(ch)], r1.at[d - 1, :, columns(ch)],
            row_send.at[7 * ch + d - 1], row_recv.at[7 * ch + d - 1], along(y2, h),
        )

    def two(ch):
        return remote(
            zs.at[:, columns(ch)], r2.at[:, columns(ch)],
            row_send.at[7 * ch + 3], row_recv.at[7 * ch + 3], along(y, 1 - h),
        )

    def three(d, ch):
        return remote(
            msg.at[d - 1, :, columns(ch)], xf.at[pl.ds(pl.multiple_of(y * part, part), part), columns(ch)],
            row_send.at[7 * ch + 3 + d], row_recv.at[7 * ch + 3 + d], along((y + d) % NY, h),
        )

    def three_in(d, ch):
        return remote(
            msg.at[d - 1, :, columns(ch)],
            xf.at[pl.ds(pl.multiple_of(((y + NY - d) % NY) * part, part), part), columns(ch)],
            row_send.at[7 * ch + 3 + d], row_recv.at[7 * ch + 3 + d], along((y + d) % NY, h),
        )

    for load in loads[1:5]:
        load.wait()
    pick(0)

    @pl.when(jnp.logical_not(is_src))
    def _():
        pl.semaphore_wait(barrier, 14)

    for ch in range(CHUNKS):
        if ch:
            pick(ch)
        for d in (2, 1, 3):
            one(d, ch).start()
        if ch == 0:
            @pl.when(first_plane & (x > 0) & (r == 0))
            def _():
                arrived(x, FIX)
                for step in (1, 2, 4, 6):
                    down(step).start()

    def goes_x(leap, t):
        return (z > 0) | (((x + leap) % NX != 0) & ((x != 2) | (leap != 1) | (t < 2)))

    def along_x(t, carry):
        for leap in (1, 3, 2):
            @pl.when(goes_x(leap, t))
            def _():
                net(x, t, 5 * leap + t, chip((x + leap) % NX, z)).start()

        return carry

    def own(t, carry):
        arrived(x, t)

        @pl.when(first_plane & (x == 3) & (t < 2))
        def _():
            arrived(2, t + 2)
            net(2, t + 2, 38 + t, chip(2, 0)).start()

        @pl.when(z < NZ - 1)
        def _():
            net(x, t, t, chip(x, z + 1)).start()

        @pl.when(z > 0)
        def _():
            along_x(t, 0)

        return carry

    def own_line(low, high):
        @pl.when(jnp.logical_not(is_src))
        def _():
            lax.fori_loop(low, high, own, 0)

    def own_fix_line():
        arrived(x, FIX)

        @pl.when(first_plane & (h == 0))
        def _():
            down(r + 1).start()

        @pl.when(first_plane)
        def _():
            for step in (3, 2, 1):
                net(x, FIX, (4, 40, 41)[step - 1], chip(x, step)).start()

        for leap in (2, 1, 3):
            net(x, FIX, 5 * leap + FIX, chip((x + leap) % NX, z)).start()

    def relayed(q, t):
        return first_plane & (x == 3) & (q == 2) & (t >= 2)

    def others(t, carry):
        for leap in (2, 1, 3):
            q = (x + leap) % NX

            @pl.when(jnp.logical_not(relayed(q, t)))
            def _():
                arrived(q, t)

        return carry

    def other_lines(low, high):
        lax.fori_loop(low, high, others, 0)

    early = (r == 1) | ((h == 0) & (r > 0))
    late = (h == 1) & (r > 1)
    own_line(0, jnp.where(z == 0, jnp.where(early, 2, jnp.where(x == 1, 3, 4)), jnp.where(z == 1, 1, 0)))
    pl.when(first_plane & early)(own_fix_line)
    own_line(jnp.where(first_plane & early, 2, 4), jnp.where(first_plane & (x == 1), 3, 4))

    home = pl.ds(pl.multiple_of(y * part, part), part)
    home_owner = wide(owner_of(pl.multiple_of(y * part, part), part), width)

    def halves(ch):
        first = jnp.zeros((part, width), jnp.float32)
        rest = jnp.zeros((part, width), jnp.float32)
        for d in range(NY):
            got = (g[home, columns(ch)] if d == 0 else r1[d - 1, :, columns(ch)]).astype(jnp.float32)
            flag = jnp.where(((y + NY - d) % NY == 0) & (h == 0), 1.0, 0.0)
            first = first + got * flag
            rest = rest + got * (1.0 - flag)
        return first, rest

    low = jnp.where(h == 0, 1, 0)
    for ch in range(CHUNKS):
        for d in (1, 3, 2):
            one(d, ch).wait_recv()
        first, rest = halves(ch)
        away = (home_owner % 2 == 0) & (home_owner != 0)
        sent_rows = jnp.where(away | (home_owner * low != home_owner), rest, jnp.where(low == 1, first, rest))
        zs[:, columns(ch)] = sent_rows.astype(jnp.bfloat16)
        two(ch).start()

    for load in loads[5:]:
        load.wait()

    def inverses():
        ub = balanced(uinv[...].astype(jnp.float32)).astype(jnp.bfloat16)
        lb = balanced(linv[...].astype(jnp.float32)).astype(jnp.bfloat16)
        both[...] = balanced(dot(ub, lb)).astype(jnp.bfloat16)

    own_line(jnp.where(first_plane & (x == 1), 3, 4), 4)
    pl.when(first_plane & late)(own_fix_line)

    @pl.when(first_plane & (x > 0))
    def _():
        lax.fori_loop(0, 4, along_x, 0)

    own_line(jnp.where(z == 0, 4, jnp.where(z == 1, 1, 0)), jnp.where(z < 2, 4, 4 - z))
    pl.when((z == 3) & (r > 0))(own_fix_line)
    own_line(jnp.where(z < 2, 4, 4 - z), jnp.where(z < 2, 4, 2))

    for ch in range(CHUNKS):
        two(ch).wait_recv()
        first, rest = halves(ch)
        got = r2[:, columns(ch)].astype(jnp.float32)
        odd = home_owner % 2 == 1
        low_t = jnp.where(odd, got, jnp.where(home_owner == 0, first, rest))
        high_t = jnp.where(odd, rest, got)
        flag = jnp.where(h == 0, 1.0, 0.0)
        new = low_t * flag + high_t * (1.0 - flag)
        old = first * flag + got * (1.0 - flag)
        for d in (2, 1, 3):
            y2 = (y + d) % NY
            msg[d - 1, :, columns(ch)] = jnp.where(home_owner == y2 * 2 + h, old, new).astype(jnp.bfloat16)
            three(d, ch).start()
        xf[home, columns(ch)] = jnp.where(home_owner == r, old, new).astype(jnp.bfloat16)

    pl.when((z > 0) & (z < 3) & (r > 0))(own_fix_line)
    own_line(jnp.where(z < 2, 4, 2), 4)
    inverses()

    @pl.when(r > 0)
    def _():
        for leap in (2, 1, 3):
            arrived((x + leap) % NX, FIX)
        core_fix().start()

    bf = jnp.bfloat16
    keep = jnp.where(c == 0, 0.0, 1.0)
    left = balanced(uinv[...].astype(jnp.float32))
    for ch in range(CHUNKS):
        for d in (1, 3, 2):
            three_in(d, ch).wait_recv()

        def finish(t, carry):
            start = pl.multiple_of(t * 128, 128)
            owner = wide(owner_of(start, 128), width)
            mine = g[pl.ds(start, 128), columns(ch)].astype(jnp.float32)
            got = xf[pl.ds(start, 128), columns(ch)].astype(jnp.float32)
            tt[pl.ds(start, 128), columns(ch)] = jnp.where(owner == r, mine, got).astype(bf)
            return carry

        lax.fori_loop(0, panel // 128, finish, 0)
        right = -balanced(dot(both[...], tt[:, columns(ch)]))
        wk[:, columns(ch)] = jnp.where(c == 0, left[:, ch * width : (ch + 1) * width], right).astype(bf)

    @pl.when(r == 0)
    def _():
        xf[...] = s_ref[0:panel, :]
        lb = balanced(linv[...].astype(jnp.float32)).astype(bf)
        upper = residue(dot(lb, tt[...]))
        out[0:panel, :] = jnp.where(c == 0, tt[...].astype(jnp.float32), upper).astype(bf)

    def swapped_in(start):
        old = xf[...].astype(jnp.float32) * keep
        rep[:, 0:panel] = residue(old + dot(pf[start : start + panel, :], wk[...])).astype(bf)
        rep[:, panel : panel + 128] = jnp.ones((panel, 128), bf)

    @pl.when(r > 0)
    def _():
        core_fix_in().wait_recv()
        swapped_in(rows)

    def write(start):
        at = pl.ds(pl.multiple_of(start, panel), panel)
        return pltpu.make_async_copy(out.at[at], o_hbm.at[at], out_sem.at[start // panel])

    def tile(start):
        at = pl.ds(pl.multiple_of(start, panel), panel)

        @pl.when((r > 0) | (start >= panel))
        def _():
            index = lax.broadcasted_iota(jnp.int32, (panel, panel), 0) + (r * rows + start)
            hit = jnp.where(index == piv_ref[...], 1.0, 0.0).astype(bf)
            swapped = dot(hit, rep[...])
            count = wide(swapped[:, panel : panel + 128], panel)
            rest = residue(s_ref[at, :].astype(jnp.float32) * keep + dot(pf[at, :], wk[...]))
            out[at, :] = jnp.where(count > 0, swapped[:, 0:panel], rest).astype(bf)

        write(start).start()

    @pl.when(is_src & (k == 0))
    def _():
        own_copy.wait()

    for i in range(2):
        @pl.when(jnp.logical_not(is_src))
        def _():
            other_lines(2 * i, 2 * i + 2)
            core_line(2 * i).start()
            core_line(2 * i + 1).start()

        def incoming():
            core_line_in(2 * i).wait_recv()
            core_line_in(2 * i + 1).wait_recv()

        from_sibling = jnp.logical_not(is_src & (k == 0))
        if i == 0:
            @pl.when(r == 0)
            def _():
                pl.when(k == 1)(incoming)
                swapped_in(0)

            from_sibling = from_sibling & ((r > 0) | (k == 0))

        def tiles(j, carry):
            @pl.when((j == 1) & from_sibling)
            def _():
                incoming()

            tile(jnp.where(j == 0, k, 1 - k) * half + i * panel)
            return carry

        lax.fori_loop(0, 2, tiles, 0)

    for t in range(4):
        write(t * panel).wait()

    for ch in range(CHUNKS):
        for d in (1, 2, 3):
            one(d, ch).wait_send()
            three(d, ch).wait_send()
        two(ch).wait_send()
    pl.when(r > 0)(lambda: core_fix().wait_send())

    @pl.when(jnp.logical_not(is_src))
    def _():
        for q in range(4):
            core_line(q).wait_send()

        def own_sent(t, carry):
            pl.when(z < NZ - 1)(lambda: sent(t))
            for leap in range(1, 4):
                pl.when(goes_x(leap, t))(lambda: sent(5 * leap + t))
            return carry

        lax.fori_loop(0, 4, own_sent, 0)

    @pl.when(first_plane & (r > 0))
    def _():
        for slot in (4, 40, 41):
            sent(slot)

    for leap in range(1, 4):
        pl.when(r > 0)(lambda: sent(5 * leap + FIX))

    @pl.when(first_plane & (x == 3))
    def _():
        sent(38)
        sent(39)

    @pl.when(is_src)
    def _():
        for slot, (q, t, x2, z2) in enumerate(plan):
            src_piece(pf, q, t, slot, chip(x2, z2)).wait_send()

        @pl.when(r == 0)
        def _():
            for q in (2, 1, 3):
                fix_out(q, 36 + q).wait_send()

        @pl.when(k == 0)
        def _():
            for q in range(4):
                give(1, q).wait_send()
                give(0, q).wait_send()

            @pl.when(r == 0)
            def _():
                give_fix().wait_send()

    @pl.when(first_plane & (r == 0))
    def _():
        for step in (1, 2, 4, 6):
            down(step).wait_send()

    @pl.when(first_plane & (r > 0) & (h == 0))
    def _():
        down(r + 1).wait_send()


def step_kernel(piv, linv, uinv, s, panel):
    rows, cols = s.shape
    part = panel // NY
    bf = jnp.bfloat16
    dma = pltpu.SemaphoreType.DMA
    anywhere = pl.BlockSpec(memory_space=pl.ANY)
    return pl.pallas_call(
        exchange_kernel,
        out_shape=jax.ShapeDtypeStruct((rows, cols), bf),
        in_specs=[pl.BlockSpec(memory_space=pltpu.HBM)] * 4,
        out_specs=anywhere,
        scratch_shapes=[
            pltpu.VMEM((1, panel), jnp.int32),
            pltpu.VMEM((panel, panel), bf),
            pltpu.VMEM((panel, panel), bf),
            pltpu.VMEM((rows, cols), bf),
            pltpu.VMEM((rows + panel, panel), bf),
            pltpu.VMEM((panel, cols), bf),
            pltpu.VMEM((panel, cols), bf),
            pltpu.VMEM((panel, panel), bf),
            pltpu.VMEM((panel, cols), bf),
            pltpu.VMEM((panel, cols + 128), bf),
            pltpu.VMEM((rows, cols), bf),
            pltpu.VMEM((panel, 128), jnp.int32),
            pltpu.VMEM((panel, rows), bf),
            pltpu.VMEM((panel, cols), bf),
            pltpu.VMEM((NY - 1, part, cols), bf),
            pltpu.VMEM((part, cols), bf),
            pltpu.VMEM((part, cols), bf),
            pltpu.VMEM((NY - 1, part, cols), bf),
            dma((42,)), dma((20,)), dma((40,)), dma((5,)), dma((5,)), dma((5,)),
            dma((7,)), dma((7 * CHUNKS,)), dma((7 * CHUNKS,)), dma((9,)), dma((4,)),
        ],
        compiler_params=pltpu.CompilerParams(
            collective_id=0, has_side_effects=True, vmem_limit_bytes=60 << 20
        ),
        name="exchange",
    )(piv, linv, uinv, s)


def divide_kernel(x_hbm, o_hbm, x, o, sem_in, sem_out):
    parts = sem_in.shape[0]
    size = x.shape[0] // parts
    spans = [pl.ds(i * size, size) for i in range(parts)]
    loads = [pltpu.make_async_copy(x_hbm.at[at], x.at[at], sem_in.at[i]) for i, at in enumerate(spans)]
    stores = [pltpu.make_async_copy(o.at[at], o_hbm.at[at], sem_out.at[i]) for i, at in enumerate(spans)]
    for load in loads:
        load.start()
    for at, load, store in zip(spans, loads, stores):
        load.wait()
        o[at, :] = x[at, :].astype(jnp.float32) * INVERSE
        store.start()
    for store in stores:
        store.wait()


def divide(x):
    anywhere = pl.BlockSpec(memory_space=pl.ANY)
    parts = 8
    return pl.pallas_call(
        divide_kernel,
        out_shape=jax.ShapeDtypeStruct(x.shape, jnp.float32),
        in_specs=[anywhere],
        out_specs=anywhere,
        scratch_shapes=[
            pltpu.VMEM(x.shape, x.dtype),
            pltpu.VMEM(x.shape, jnp.float32),
            pltpu.SemaphoreType.DMA((parts,)),
            pltpu.SemaphoreType.DMA((parts,)),
        ],
        compiler_params=pltpu.CompilerParams(vmem_limit_bytes=60 << 20),
        name="divide",
    )(x)


def per_device(matrix, pivots, lower_inverse, upper_inverse):
    panel = lower_inverse.shape[0]
    piv = pivots.reshape(1, panel)
    return divide(step_kernel(piv, lower_inverse, upper_inverse, matrix, panel))


def solution(mesh):
    placed = (P("row", "col"), P(), P(), P())
    return jax.shard_map(
        per_device, mesh=mesh, in_specs=placed, out_specs=P("row", "col"), check_vma=False
    )
```

```python
import functools

import jax
import jax.numpy as jnp
from jax import lax
from jax.experimental import pallas as pl
from jax.experimental.pallas import tpu as pltpu
from jax.sharding import PartitionSpec as P

MESH = pl.DeviceIdType.MESH
PRIME = 251.0
INVERSE = 1.0 / 251.0
ROUND = 1.5 * 2.0**23
NY, NX, NZ = 4, 4, 4
CHUNKS = 2
FIX = 4


def balanced(x):
    quot = (x * INVERSE + ROUND) - ROUND
    return x - quot * PRIME


def residue(x):
    rest = balanced(x)
    return jnp.where(rest < 0, rest + PRIME, rest)


def dot(a, b):
    return jnp.dot(a, b, preferred_element_type=jnp.float32)


def exchange_kernel(
    piv_hbm, linv_hbm, uinv_hbm, s_hbm, o_hbm, piv_ref, linv, uinv, out, hits, pf, tt, xf, both, wk, rep, s_ref, pcol, oh, g, r1, zs, r2, msg,
    net_send, net_recv, src_send, src_recv, core_send, core_recv, down_send, row_send, row_recv, loc, out_sem,
):
    rows = s_ref.shape[0]
    panel = xf.shape[0]
    half = rows // 2
    line = half // NX
    piece = line // 4
    fix = panel // 2
    part = panel // NY
    r = lax.axis_index("row")
    c = lax.axis_index("col")
    y, h = r // 2, r % 2
    x, z, k = c // 8, (c // 2) % 4, c % 2
    first_plane = z == 0
    is_src = first_plane & (x == 0)
    quarter = rows // 4
    spans = [pl.ds(i * quarter, quarter) for i in range(4)]
    pairs = [(piv_hbm, piv_ref)]
    pairs += [(s_hbm.at[at], s_ref.at[at]) for at in spans]
    pairs += [(uinv_hbm, uinv), (linv_hbm, linv)]
    loads = [
        pltpu.make_async_copy(src, dst, loc.at[2 + i]) for i, (src, dst) in enumerate(pairs)
    ]
    for load in loads:
        load.start()

    def chip(x2, z2):
        return {"row": r, "col": x2 * 8 + z2 * 2 + k}

    def along(y2, h2):
        return {"row": y2 * 2 + h2, "col": c}

    sibling = {"row": r, "col": c + 1 - 2 * k}
    barrier = pltpu.get_barrier_semaphore()

    def signal(device):
        pl.semaphore_signal(barrier, 1, device_id=device, device_id_type=MESH)

    signal(sibling)
    for step in range(1, 4):
        signal(chip((x + step) % NX, z))
        signal(chip(x, (z + step) % NZ))
    for step in range(1, 8):
        signal({"row": (r + step) % 8, "col": c})

    def remote(src, dst, send, recv, device):
        return pltpu.make_async_remote_copy(
            src_ref=src, dst_ref=dst, send_sem=send, recv_sem=recv,
            device_id=device, device_id_type=MESH,
        )

    def place(q, t):
        if isinstance(t, int) and t == FIX:
            return pl.ds(pl.multiple_of(rows + k * fix + q * piece, piece), piece)
        return pl.ds(pl.multiple_of(k * half + t * line + q * piece, piece), piece)

    def net(q, t, slot, device):
        return remote(
            pf.at[place(q, t)], pf.at[place(q, t)], net_send.at[slot], net_recv.at[q * 5 + t], device
        )

    def arrived(q, t):
        net(q, t, 0, sibling).wait_recv()

    def sent(slot):
        net(0, 0, slot, sibling).wait_send()

    def src_piece(ref, q, t, slot, device):
        return remote(
            ref.at[place(q, t)], pf.at[place(q, t)], src_send.at[slot], net_recv.at[q * 5 + t], device
        )

    def line_place(k2, q):
        return pl.ds(pl.multiple_of(k2 * half + q * line, line), line)

    def core_line(q):
        return remote(
            pf.at[line_place(k, q)], pf.at[line_place(k, q)], core_send.at[q], core_recv.at[q], sibling
        )

    def core_line_in(q):
        return remote(
            pf.at[line_place(1 - k, q)], pf.at[line_place(1 - k, q)],
            core_send.at[q], core_recv.at[q], sibling,
        )

    def fix_place(k2):
        return pl.ds(pl.multiple_of(rows + k2 * fix, fix), fix)

    def core_fix():
        return remote(
            pf.at[fix_place(k)], pf.at[fix_place(k)], core_send.at[4], core_recv.at[4], sibling
        )

    def core_fix_in():
        return remote(
            pf.at[fix_place(1 - k)], pf.at[fix_place(1 - k)],
            core_send.at[4], core_recv.at[4], sibling,
        )

    def give(k2, q):
        at = pl.ds(k2 * half + q * line, line)
        return remote(
            s_hbm.at[at], pf.at[at], src_send.at[28 + k2 * 4 + q],
            src_recv.at[q] if k2 else core_recv.at[q], sibling,
        )

    def give_fix():
        return remote(
            s_hbm.at[pl.ds(fix, fix)], pf.at[pl.ds(rows + fix, fix)],
            src_send.at[36], src_recv.at[4], sibling,
        )

    own_copy = pltpu.make_async_copy(s_hbm, pf.at[pl.ds(0, rows)], loc.at[0])
    own_fix = pltpu.make_async_copy(s_hbm.at[pl.ds(0, fix)], pf.at[pl.ds(rows, fix)], loc.at[1])

    def fix_out(q, slot):
        return remote(
            pf.at[place(q, 4)], pf.at[place(q, 4)], src_send.at[slot], net_recv.at[q * 5 + 4], chip(q, 0)
        )

    def down(step):
        return remote(
            pf.at[place(x, FIX)], pf.at[place(x, FIX)], down_send.at[step // 2 if isinstance(step, int) else 0],
            net_recv.at[x * 5 + FIX], {"row": step, "col": c},
        )

    plan = (
        (2, 0, 2, 0), (3, 0, 3, 0), (0, 0, 0, 1), (1, 0, 1, 0), (2, 2, 3, 0), (0, 1, 0, 1),
        (2, 1, 2, 0), (3, 1, 3, 0), (1, 1, 1, 0), (2, 3, 3, 0), (0, 2, 0, 1),
        (1, 2, 1, 0), (3, 2, 3, 0), (0, 3, 0, 1), (1, 3, 1, 0), (3, 3, 3, 0),
    ) + tuple((0, t, x2, 0) for t in range(4) for x2 in (1, 3, 2))

    def fix_sends():
        for q in (2, 1, 3):
            fix_out(q, 36 + q).start()
        for step in (1, 2, 4, 6):
            down(step).start()

    @pl.when(is_src)
    def _():
        pl.semaphore_wait(barrier, 14)

        @pl.when(k == 0)
        def _():
            @pl.when(r == 0)
            def _():
                give_fix().start()
                own_fix.start()

            for q in (0, 2, 1, 3):
                give(1, q).start()

            @pl.when(r == 0)
            def _():
                own_fix.wait()
                fix_sends()

            for slot, (q, t, x2, z2) in enumerate(plan):
                src_piece(s_hbm, q, t, slot, chip(x2, z2)).start()

            own_copy.start()
            for q in range(4):
                give(0, q).start()

        @pl.when(k == 1)
        def _():
            @pl.when(r == 0)
            def _():
                remote(
                    pf.at[fix_place(1)], pf.at[fix_place(1)], src_send.at[36], src_recv.at[4], sibling
                ).wait_recv()
                fix_sends()

            ready = []
            for slot, (q, t, x2, z2) in enumerate(plan):
                if t not in ready:
                    ready.append(t)
                    remote(
                        pf.at[line_place(1, t)], pf.at[line_place(1, t)],
                        src_send.at[28 + t], src_recv.at[t], sibling,
                    ).wait_recv()
                src_piece(pf, q, t, slot, chip(x2, z2)).start()

    loads[0].wait()
    lane = lax.broadcasted_iota(jnp.int32, (panel, 128), 1)
    for t in range(panel // 128):
        wide_line = jnp.broadcast_to(piv_ref[:, t * 128 : (t + 1) * 128], (128, 128))
        pcol[t * 128 : (t + 1) * 128, :] = jnp.transpose(wide_line)
    named = pcol[...]

    def build(t, carry):
        hit = named == lane + (r * rows + t * 128)
        oh[:, pl.ds(pl.multiple_of(t * 128, 128), 128)] = jnp.where(hit, 1.0, 0.0).astype(jnp.bfloat16)
        return carry

    lax.fori_loop(0, rows // 128, build, 0)

    def owner_of(start, size):
        return pcol[pl.ds(start, size), :] // rows

    def wide(mask_value, width):
        return jnp.concatenate([mask_value] * (width // 128), axis=1)

    width = s_ref.shape[1] // CHUNKS

    def columns(ch):
        return pl.ds(ch * width, width)

    def pick(ch):
        def body(t, carry):
            start = pl.multiple_of(t * 256, 256)
            picked = dot(oh[pl.ds(start, 256), :], s_ref[:, columns(ch)])
            owner = wide(owner_of(start, 256), width)
            old = s_ref[pl.ds(start, 256), columns(ch)].astype(jnp.float32)
            use = (owner * jnp.where(r == 0, 1, 0)) == 0
            g[pl.ds(start, 256), columns(ch)] = jnp.where(use, picked, old).astype(jnp.bfloat16)
            return carry

        lax.fori_loop(0, panel // 256, body, 0)

    def one(d, ch):
        y2 = (y + d) % NY
        return remote(
            g.at[pl.ds(pl.multiple_of(y2 * part, part), part), columns(ch)], r1.at[d - 1, :, columns(ch)],
            row_send.at[7 * ch + d - 1], row_recv.at[7 * ch + d - 1], along(y2, h),
        )

    def two(ch):
        return remote(
            zs.at[:, columns(ch)], r2.at[:, columns(ch)],
            row_send.at[7 * ch + 3], row_recv.at[7 * ch + 3], along(y, 1 - h),
        )

    def three(d, ch):
        return remote(
            msg.at[d - 1, :, columns(ch)], xf.at[pl.ds(pl.multiple_of(y * part, part), part), columns(ch)],
            row_send.at[7 * ch + 3 + d], row_recv.at[7 * ch + 3 + d], along((y + d) % NY, h),
        )

    def three_in(d, ch):
        return remote(
            msg.at[d - 1, :, columns(ch)],
            xf.at[pl.ds(pl.multiple_of(((y + NY - d) % NY) * part, part), part), columns(ch)],
            row_send.at[7 * ch + 3 + d], row_recv.at[7 * ch + 3 + d], along((y + d) % NY, h),
        )

    for load in loads[1:5]:
        load.wait()
    pick(0)

    @pl.when(jnp.logical_not(is_src))
    def _():
        pl.semaphore_wait(barrier, 14)

    for ch in range(CHUNKS):
        if ch:
            pick(ch)
        for d in (2, 1, 3):
            one(d, ch).start()
        if ch == 0:
            @pl.when(first_plane & (x > 0) & (r == 0))
            def _():
                arrived(x, FIX)
                for step in (1, 2, 4, 6):
                    down(step).start()

    def goes_x(leap, t):
        return (z > 0) | (((x + leap) % NX != 0) & ((x != 2) | (leap != 1) | (t < 2)))

    def along_x(t, carry):
        for leap in (1, 3, 2):
            @pl.when(goes_x(leap, t))
            def _():
                net(x, t, 5 * leap + t, chip((x + leap) % NX, z)).start()

        return carry

    def own(t, carry):
        arrived(x, t)

        @pl.when(first_plane & (x == 3) & (t < 2))
        def _():
            arrived(2, t + 2)
            net(2, t + 2, 38 + t, chip(2, 0)).start()

        @pl.when(z < NZ - 1)
        def _():
            net(x, t, t, chip(x, z + 1)).start()

        @pl.when(z > 0)
        def _():
            along_x(t, 0)

        return carry

    def own_line(low, high):
        @pl.when(jnp.logical_not(is_src))
        def _():
            lax.fori_loop(low, high, own, 0)

    def own_fix_line():
        arrived(x, FIX)

        @pl.when(first_plane & (h == 0))
        def _():
            down(r + 1).start()

        @pl.when(first_plane)
        def _():
            for step in (3, 2, 1):
                net(x, FIX, (4, 40, 41)[step - 1], chip(x, step)).start()

        for leap in (2, 1, 3):
            net(x, FIX, 5 * leap + FIX, chip((x + leap) % NX, z)).start()

    def relayed(q, t):
        return first_plane & (x == 3) & (q == 2) & (t >= 2)

    def others(t, carry):
        for leap in (2, 1, 3):
            q = (x + leap) % NX

            @pl.when(jnp.logical_not(relayed(q, t)))
            def _():
                arrived(q, t)

        return carry

    def other_lines(low, high):
        lax.fori_loop(low, high, others, 0)

    early = (r == 1) | ((h == 0) & (r > 0))
    late = (h == 1) & (r > 1)
    own_line(0, jnp.where(z == 0, jnp.where(early, 2, jnp.where(x == 1, 3, 4)), jnp.where(z == 1, 1, 0)))
    pl.when(first_plane & early)(own_fix_line)
    own_line(jnp.where(first_plane & early, 2, 4), jnp.where(first_plane & (x == 1), 3, 4))

    home = pl.ds(pl.multiple_of(y * part, part), part)
    home_owner = wide(owner_of(pl.multiple_of(y * part, part), part), width)

    def halves(ch):
        first = jnp.zeros((part, width), jnp.float32)
        rest = jnp.zeros((part, width), jnp.float32)
        for d in range(NY):
            got = (g[home, columns(ch)] if d == 0 else r1[d - 1, :, columns(ch)]).astype(jnp.float32)
            flag = jnp.where(((y + NY - d) % NY == 0) & (h == 0), 1.0, 0.0)
            first = first + got * flag
            rest = rest + got * (1.0 - flag)
        return first, rest

    low = jnp.where(h == 0, 1, 0)
    for ch in range(CHUNKS):
        for d in (1, 3, 2):
            one(d, ch).wait_recv()
        first, rest = halves(ch)
        away = (home_owner % 2 == 0) & (home_owner != 0)
        sent_rows = jnp.where(away | (home_owner * low != home_owner), rest, jnp.where(low == 1, first, rest))
        zs[:, columns(ch)] = sent_rows.astype(jnp.bfloat16)
        two(ch).start()

    for load in loads[5:]:
        load.wait()

    def inverses():
        ub = balanced(uinv[...].astype(jnp.float32)).astype(jnp.bfloat16)
        lb = balanced(linv[...].astype(jnp.float32)).astype(jnp.bfloat16)
        both[...] = balanced(dot(ub, lb)).astype(jnp.bfloat16)

    own_line(jnp.where(first_plane & (x == 1), 3, 4), 4)
    pl.when(first_plane & late)(own_fix_line)

    @pl.when(first_plane & (x > 0))
    def _():
        lax.fori_loop(0, 4, along_x, 0)

    own_line(jnp.where(z == 0, 4, jnp.where(z == 1, 1, 0)), jnp.where(z < 2, 4, 4 - z))
    pl.when((z == 3) & (r > 0))(own_fix_line)
    own_line(jnp.where(z < 2, 4, 4 - z), jnp.where(z < 2, 4, 2))

    for ch in range(CHUNKS):
        two(ch).wait_recv()
        first, rest = halves(ch)
        got = r2[:, columns(ch)].astype(jnp.float32)
        odd = home_owner % 2 == 1
        low_t = jnp.where(odd, got, jnp.where(home_owner == 0, first, rest))
        high_t = jnp.where(odd, rest, got)
        flag = jnp.where(h == 0, 1.0, 0.0)
        new = low_t * flag + high_t * (1.0 - flag)
        old = first * flag + got * (1.0 - flag)
        for d in (2, 1, 3):
            y2 = (y + d) % NY
            msg[d - 1, :, columns(ch)] = jnp.where(home_owner == y2 * 2 + h, old, new).astype(jnp.bfloat16)
            three(d, ch).start()
        xf[home, columns(ch)] = jnp.where(home_owner == r, old, new).astype(jnp.bfloat16)

    pl.when((z > 0) & (z < 3) & (r > 0))(own_fix_line)
    own_line(jnp.where(z < 2, 4, 2), 4)
    inverses()

    def mark(t, carry):
        start = pl.multiple_of(t * 128, 128)
        index = lax.broadcasted_iota(jnp.int32, (128, panel), 0) + (r * rows + start)
        hits[pl.ds(start, 128), :] = jnp.where(index == piv_ref[...], 1.0, 0.0).astype(jnp.bfloat16)
        return carry

    lax.fori_loop(0, rows // 128, mark, 0)

    @pl.when(r > 0)
    def _():
        for leap in (2, 1, 3):
            arrived((x + leap) % NX, FIX)
        core_fix().start()

    bf = jnp.bfloat16
    keep = jnp.where(c == 0, 0.0, 1.0)
    left = balanced(uinv[...].astype(jnp.float32))
    for ch in range(CHUNKS):
        for d in (1, 3, 2):
            three_in(d, ch).wait_recv()

        def finish(t, carry):
            start = pl.multiple_of(t * 128, 128)
            owner = wide(owner_of(start, 128), width)
            mine = g[pl.ds(start, 128), columns(ch)].astype(jnp.float32)
            got = xf[pl.ds(start, 128), columns(ch)].astype(jnp.float32)
            tt[pl.ds(start, 128), columns(ch)] = jnp.where(owner == r, mine, got).astype(bf)
            return carry

        lax.fori_loop(0, panel // 128, finish, 0)
        right = -balanced(dot(both[...], tt[:, columns(ch)]))
        wk[:, columns(ch)] = jnp.where(c == 0, left[:, ch * width : (ch + 1) * width], right).astype(bf)

    @pl.when(r == 0)
    def _():
        xf[...] = s_ref[0:panel, :]
        lb = balanced(linv[...].astype(jnp.float32)).astype(bf)
        upper = residue(dot(lb, tt[...]))
        out[0:panel, :] = jnp.where(c == 0, tt[...].astype(jnp.float32), upper).astype(bf)

    def swapped_in(start):
        old = xf[...].astype(jnp.float32) * keep
        rep[:, 0:panel] = residue(old + dot(pf[start : start + panel, :], wk[...])).astype(bf)
        rep[:, panel : panel + 128] = jnp.ones((panel, 128), bf)

    @pl.when(r > 0)
    def _():
        core_fix_in().wait_recv()
        swapped_in(rows)

    def write(start):
        at = pl.ds(pl.multiple_of(start, panel), panel)
        return pltpu.make_async_copy(out.at[at], o_hbm.at[at], out_sem.at[start // panel])

    def tile(start):
        at = pl.ds(pl.multiple_of(start, panel), panel)

        @pl.when((r > 0) | (start >= panel))
        def _():
            swapped = dot(hits[at, :], rep[...])
            count = wide(swapped[:, panel : panel + 128], panel)
            rest = residue(s_ref[at, :].astype(jnp.float32) * keep + dot(pf[at, :], wk[...]))
            out[at, :] = jnp.where(count > 0, swapped[:, 0:panel], rest).astype(bf)

        write(start).start()

    @pl.when(is_src & (k == 0))
    def _():
        own_copy.wait()

    for i in range(2):
        @pl.when(jnp.logical_not(is_src))
        def _():
            other_lines(2 * i, 2 * i + 2)
            core_line(2 * i).start()
            core_line(2 * i + 1).start()

        def incoming():
            core_line_in(2 * i).wait_recv()
            core_line_in(2 * i + 1).wait_recv()

        from_sibling = jnp.logical_not(is_src & (k == 0))
        if i == 0:
            @pl.when(r == 0)
            def _():
                pl.when(k == 1)(incoming)
                swapped_in(0)

            from_sibling = from_sibling & ((r > 0) | (k == 0))

        def tiles(j, carry):
            @pl.when((j == 1) & from_sibling)
            def _():
                incoming()

            tile(jnp.where(j == 0, k, 1 - k) * half + i * panel)
            return carry

        lax.fori_loop(0, 2, tiles, 0)

    for t in range(4):
        write(t * panel).wait()

    for ch in range(CHUNKS):
        for d in (1, 2, 3):
            one(d, ch).wait_send()
            three(d, ch).wait_send()
        two(ch).wait_send()
    pl.when(r > 0)(lambda: core_fix().wait_send())

    @pl.when(jnp.logical_not(is_src))
    def _():
        for q in range(4):
            core_line(q).wait_send()

        def own_sent(t, carry):
            pl.when(z < NZ - 1)(lambda: sent(t))
            for leap in range(1, 4):
                pl.when(goes_x(leap, t))(lambda: sent(5 * leap + t))
            return carry

        lax.fori_loop(0, 4, own_sent, 0)

    @pl.when(first_plane & (r > 0))
    def _():
        for slot in (4, 40, 41):
            sent(slot)

    for leap in range(1, 4):
        pl.when(r > 0)(lambda: sent(5 * leap + FIX))

    @pl.when(first_plane & (x == 3))
    def _():
        sent(38)
        sent(39)

    @pl.when(is_src)
    def _():
        for slot, (q, t, x2, z2) in enumerate(plan):
            src_piece(pf, q, t, slot, chip(x2, z2)).wait_send()

        @pl.when(r == 0)
        def _():
            for q in (2, 1, 3):
                fix_out(q, 36 + q).wait_send()

        @pl.when(k == 0)
        def _():
            for q in range(4):
                give(1, q).wait_send()
                give(0, q).wait_send()

            @pl.when(r == 0)
            def _():
                give_fix().wait_send()

    @pl.when(first_plane & (r == 0))
    def _():
        for step in (1, 2, 4, 6):
            down(step).wait_send()

    @pl.when(first_plane & (r > 0) & (h == 0))
    def _():
        down(r + 1).wait_send()


def step_kernel(piv, linv, uinv, s, panel):
    rows, cols = s.shape
    part = panel // NY
    bf = jnp.bfloat16
    dma = pltpu.SemaphoreType.DMA
    anywhere = pl.BlockSpec(memory_space=pl.ANY)
    return pl.pallas_call(
        exchange_kernel,
        out_shape=jax.ShapeDtypeStruct((rows, cols), bf),
        in_specs=[pl.BlockSpec(memory_space=pltpu.HBM)] * 4,
        out_specs=anywhere,
        scratch_shapes=[
            pltpu.VMEM((1, panel), jnp.int32),
            pltpu.VMEM((panel, panel), bf),
            pltpu.VMEM((panel, panel), bf),
            pltpu.VMEM((rows, cols), bf),
            pltpu.VMEM((rows, panel), bf),
            pltpu.VMEM((rows + panel, panel), bf),
            pltpu.VMEM((panel, cols), bf),
            pltpu.VMEM((panel, cols), bf),
            pltpu.VMEM((panel, panel), bf),
            pltpu.VMEM((panel, cols), bf),
            pltpu.VMEM((panel, cols + 128), bf),
            pltpu.VMEM((rows, cols), bf),
            pltpu.VMEM((panel, 128), jnp.int32),
            pltpu.VMEM((panel, rows), bf),
            pltpu.VMEM((panel, cols), bf),
            pltpu.VMEM((NY - 1, part, cols), bf),
            pltpu.VMEM((part, cols), bf),
            pltpu.VMEM((part, cols), bf),
            pltpu.VMEM((NY - 1, part, cols), bf),
            dma((42,)), dma((20,)), dma((40,)), dma((5,)), dma((5,)), dma((5,)),
            dma((7,)), dma((7 * CHUNKS,)), dma((7 * CHUNKS,)), dma((9,)), dma((4,)),
        ],
        compiler_params=pltpu.CompilerParams(
            collective_id=0, has_side_effects=True, vmem_limit_bytes=60 << 20
        ),
        name="exchange",
    )(piv, linv, uinv, s)


def divide_kernel(x_hbm, o_hbm, x, o, sem_in, sem_out):
    parts = sem_in.shape[0]
    size = x.shape[0] // parts
    spans = [pl.ds(i * size, size) for i in range(parts)]
    loads = [pltpu.make_async_copy(x_hbm.at[at], x.at[at], sem_in.at[i]) for i, at in enumerate(spans)]
    stores = [pltpu.make_async_copy(o.at[at], o_hbm.at[at], sem_out.at[i]) for i, at in enumerate(spans)]
    for load in loads:
        load.start()
    for at, load, store in zip(spans, loads, stores):
        load.wait()
        o[at, :] = x[at, :].astype(jnp.float32) * INVERSE
        store.start()
    for store in stores:
        store.wait()


def divide(x):
    anywhere = pl.BlockSpec(memory_space=pl.ANY)
    parts = 8
    return pl.pallas_call(
        divide_kernel,
        out_shape=jax.ShapeDtypeStruct(x.shape, jnp.float32),
        in_specs=[anywhere],
        out_specs=anywhere,
        scratch_shapes=[
            pltpu.VMEM(x.shape, x.dtype),
            pltpu.VMEM(x.shape, jnp.float32),
            pltpu.SemaphoreType.DMA((parts,)),
            pltpu.SemaphoreType.DMA((parts,)),
        ],
        compiler_params=pltpu.CompilerParams(vmem_limit_bytes=60 << 20),
        name="divide",
    )(x)


def per_device(matrix, pivots, lower_inverse, upper_inverse):
    panel = lower_inverse.shape[0]
    piv = pivots.reshape(1, panel)
    return divide(step_kernel(piv, lower_inverse, upper_inverse, matrix, panel))


def solution(mesh):
    placed = (P("row", "col"), P(), P(), P())
    return jax.shard_map(
        per_device, mesh=mesh, in_specs=placed, out_specs=P("row", "col"), check_vma=False
    )
```
